32 devices in a mesh: group: 2 (over y), gx: 4 (over z), gy: 4 (over x, core).
Axes of the slice: x: 2, y: 2, z: 4, core: 2. Of those that a mesh axis runs over, the one named last changes fastest.
Arguments:
- positions: float32 [3, 8, 4, 256], P(None, ('group', 'gx'), 'gy'), parts along dimension 1
- species: int32 [8, 4, 256], P(('group', 'gx'), 'gy'), parts along dimension 0, may hold values from 0 to 7
- neighbours: int32 [8, 4, 64, 256], P(('group', 'gx'), 'gy'), parts along dimension 0, may hold values from 0 to 1279, as said below
- counts: int32 [8, 4, 256], P(('group', 'gx'), 'gy'), parts along dimension 0, may hold values from 8 to 64, as said below
- ghost_list: int32 [8, 4, 8, 128], P(('group', 'gx'), 'gy'), parts along dimension 0, may hold values from 0 to 255, as said below
- wave_index: int32 [3, 2048], replicated, may hold values from -4 to 26, as said below
- embedding: float32 [8, 64], replicated, may hold values from -6 to 6
- radial_weight: float32 [8, 64], replicated, may hold values from -2 to 2
- product_weight: float32 [128, 64], replicated, may hold values from -0.5 to 0.5
- readout_weight: float32 [64], replicated, may hold values from -0.75 to 0.75
- charge_weight: float32 [64, 64], replicated, may hold values from -0.75 to 0.75
Outputs:
- forces: float32 [3, 8, 4, 256], P(None, ('group', 'gx'), 'gy'), parts along dimension 1
- site_energy: float32 [8, 4, 256], P(('group', 'gx'), 'gy'), parts along dimension 0
The draws below stay inside these ranges and needn't reach their ends.
There are 2 independent parts, one for each index of `group`. The reference program is written for one: setup_inputs(seed, part) draws one part's arguments, and reference() takes and returns one part's arrays. A program takes and returns all parts, laid end to end along the dimension named above; an argument that names none is the same for every part. Nothing has to cross between parts.
Inputs may be any that keep to these rules, and one draw needn't show every extreme that they name: `neighbours`: an entry below 256 is an own atom of the domain, else ghost column entry - 256 of step one; never the atom itself. `counts`: slots at or beyond an atom's count are padding. `ghost_list`: atoms of the sending domain. `wave_index`: the 2048 k-vectors are distinct; first row from -4 to 4, second from -4 to 4, third from 1 to 26.
All inputs are finite; a program needn't handle non-finite values.
Results may differ from the reference program's by a relative error of at most 0.0003.
Values sent between devices are 32-bit elements; how exact they have to be, the bound alone decides.
A program may use at most 64 MiB of HBM per device.

```python
import math
import jax
import jax.numpy as jnp
from jax import lax

C = 64
NSPEC = 8
NRBF = 8
NB = 64
K = 2048
A = 256
G = 128
DOMX = 4
DOMY = 4
KXR = 4
KYR = 4
KZR = 26


def draw_positions(key, part):
    key = jax.random.fold_in(key, 1)
    key_plane, key_height = jax.random.split(key)
    lateral = jax.random.uniform(key_plane, (2, DOMX, DOMY, A), jnp.float32)
    uniform_height = jax.random.uniform(key_height, (1, DOMX, DOMY, A), jnp.float32)
    height = 1.999 * uniform_height
    return jnp.concatenate([lateral, height], axis=0)


def draw_neighbours(key, part):
    key = jax.random.fold_in(key, 2)
    extent = A + 8 * G
    offsets = jax.random.randint(key, (DOMX, DOMY, NB, A), 1, extent)
    atom_ids = lax.broadcasted_iota(jnp.int32, (DOMX, DOMY, NB, A), 3)
    codes = (atom_ids + offsets) % extent
    codes = codes.at[:, :, 0, 0].set(extent - 1)
    codes = codes.at[:, :, 1, 1].set(0)
    return codes


def draw_counts(key, part):
    key = jax.random.fold_in(key, 3)
    column = jnp.arange(DOMX, dtype=jnp.int32)
    upper = NB // 4 + 3 * NB // 4 * column // (DOMX - 1)
    lower = upper // 2
    upper_full = jnp.broadcast_to(upper[:, None, None], (DOMX, DOMY, A))
    lower_full = jnp.broadcast_to(lower[:, None, None], (DOMX, DOMY, A))
    drawn = jax.random.randint(key, (DOMX, DOMY, A), lower_full, upper_full + 1)
    drawn = drawn.at[:, :, 0].set(upper_full[:, :, 0])
    drawn = drawn.at[:, :, 1].set(lower_full[:, :, 1])
    return drawn


def draw_ghost_list(key, part):
    key = jax.random.fold_in(key, 4)
    drawn = jax.random.randint(key, (DOMX, DOMY, 8, G), 0, A)
    drawn = drawn.at[:, :, 0, 0].set(A - 1)
    drawn = drawn.at[:, :, 0, 1].set(0)
    return drawn


def draw_wave_index(key, part):
    key = jax.random.fold_in(key, 5)
    span_y = 2 * KYR + 1
    plane_size = (2 * KXR + 1) * span_y
    lattice = plane_size * KZR
    inner_codes = jax.random.permutation(key, lattice - 2)[:K - 2].astype(jnp.int32) + 1
    lattice_codes = jnp.concatenate([jnp.zeros((1,), jnp.int32), jnp.full((1,), lattice - 1, jnp.int32), inner_codes])
    index_z = lattice_codes // plane_size + 1
    remainder = lattice_codes % plane_size
    index_x = remainder // span_y - KXR
    index_y = remainder % span_y - KYR
    return jnp.stack([index_x, index_y, index_z]).astype(jnp.int32)


def with_ends(entries, rng, least, top_value):
    place = [jax.random.randint(jax.random.fold_in(rng, axis), (), 0, length) for axis, length in enumerate(entries.shape)]
    longest = entries.shape.index(max(entries.shape))
    neighbour = place[:longest] + [(place[longest] + 1) % entries.shape[longest]] + place[longest + 1:]
    return entries.at[tuple(place)].set(least).at[tuple(neighbour)].set(top_value)


def noise(own_key, dims, width, reach, kind=jnp.bfloat16):
    return jnp.clip(width * jax.random.normal(own_key, dims, jnp.float32), -reach, reach).astype(kind)


def setup_inputs(seed: int = 0, part: int = 0) -> dict:
    keys = jax.random.split(jax.random.key(seed), 12)
    part_splits = jax.random.split(jax.random.fold_in(keys[11], part), 12)
    return {
        "positions": draw_positions(jax.random.fold_in(jax.random.fold_in(keys[11], part), 71), part),
        "species": with_ends(jax.random.randint(part_splits[1], (DOMX, DOMY, A), 0, NSPEC), jax.random.fold_in(part_splits[1], 1), 0, NSPEC - 1).astype(jnp.int32),
        "neighbours": draw_neighbours(jax.random.fold_in(jax.random.fold_in(keys[11], part), 71), part),
        "counts": draw_counts(jax.random.fold_in(jax.random.fold_in(keys[11], part), 71), part),
        "ghost_list": draw_ghost_list(jax.random.fold_in(jax.random.fold_in(keys[11], part), 71), part),
        "wave_index": draw_wave_index(jax.random.fold_in(keys[11], 71), part),
        "embedding": noise(keys[6], (NSPEC, C), 1.0, 6.0, jnp.float32),
        "radial_weight": noise(keys[7], (NRBF, C), NRBF ** -0.5, 2.0, jnp.float32),
        "product_weight": noise(keys[8], (2 * C, C), (2 * C) ** -0.5, 0.5, jnp.float32),
        "readout_weight": noise(keys[9], (C,), C ** -0.5, 0.75, jnp.float32),
        "charge_weight": noise(keys[10], (C, C), C ** -0.5, 0.75, jnp.float32),
    }


DIRECTIONS = ((-1, -1), (-1, 0), (-1, 1), (0, -1), (0, 1), (1, -1), (1, 0), (1, 1))
SOFTENING = 0.01
BASIS_WIDTH = 2.0
BASIS_STEP = 0.35
SCREENING = 0.02
SLAB_HEIGHT = 2.0
PRECISE = lax.Precision.HIGHEST

def short_range(ext_pos, ext_kind, neighbour_codes, slot_counts, embedding, radial_weight, product_weight, readout_weight, charge_weight):
    atom_count = neighbour_codes.shape[1]
    slot_count = neighbour_codes.shape[0]
    channels = embedding.shape[1]
    centre = ext_pos[:, :atom_count]
    nearby = jnp.take(ext_pos, neighbour_codes, axis=1)
    near_kind = jnp.take(ext_kind, neighbour_codes, axis=0)
    separation = nearby - centre[:, None, :]
    radius = jnp.sqrt(lax.optimization_barrier(jnp.sum(separation * separation, axis=0)) + SOFTENING)
    unit_vector = separation / radius[None]
    slot_index = lax.broadcasted_iota(jnp.int32, neighbour_codes.shape, 0)
    live_mask = (slot_index < slot_counts[None, :]).astype(ext_pos.dtype)
    centres = BASIS_STEP * jnp.arange(radial_weight.shape[0]).astype(ext_pos.dtype)
    radial = jnp.exp(-BASIS_WIDTH * jnp.square(radius[None] - centres[:, None, None])) * live_mask[None]
    species_ids = jnp.arange(embedding.shape[0]).astype(ext_pos.dtype)
    near_onehot = (near_kind[None] == species_ids[:, None, None]).astype(ext_pos.dtype)
    own_onehot = (ext_kind[:atom_count][None] == species_ids[:, None]).astype(ext_pos.dtype)
    density = jnp.einsum('bna,sna->bsa', radial, near_onehot, precision=PRECISE)
    oriented = unit_vector[:, None] * radial[None]
    polar_sum = jnp.einsum('xbna,sna->xbsa', oriented, near_onehot, precision=PRECISE)
    mixing = (radial_weight[:, None, :] * embedding[None, :, :]).reshape(-1, channels)
    norm_factor = 1.0 / math.sqrt(slot_count)
    scalar = norm_factor * jnp.dot(mixing.T, density.reshape(-1, atom_count), precision=PRECISE)
    scalar = scalar + jnp.dot(embedding.T, own_onehot, precision=PRECISE)
    vectorial = norm_factor * jnp.einsum('kc,xka->xca', mixing, polar_sum.reshape(3, -1, atom_count), precision=PRECISE)
    invariants = jnp.concatenate([scalar, lax.optimization_barrier(jnp.sum(vectorial * vectorial, axis=0))], axis=0)
    hidden = jax.nn.silu(jnp.dot(product_weight.T, invariants, precision=PRECISE))
    short_energy = jnp.dot(readout_weight, hidden, precision=PRECISE)
    charges = jnp.dot(charge_weight.T, scalar, precision=PRECISE)
    return (short_energy, charges)

def wave_table(wave_index, span_x, span_y):
    lengths = jnp.array([span_x, span_y, SLAB_HEIGHT], jnp.float32)
    return 2.0 * math.pi * wave_index.astype(jnp.float32) / lengths[:, None]

def wave_weight(wave_vectors):
    squared = lax.optimization_barrier(jnp.sum(wave_vectors * wave_vectors, axis=0))
    return jnp.exp(-0.5 * SCREENING * SCREENING * squared) / (squared + 1.0)

def reference(positions, species, neighbours, counts, ghost_list, wave_index, embedding, radial_weight, product_weight, readout_weight, charge_weight):
    dom_x, dom_y, atom_count = species.shape
    ghost_width = ghost_list.shape[3]
    domains = dom_x * dom_y
    record = jnp.concatenate([positions, species.astype(jnp.float32)[None]], axis=0)
    arrivals = []
    for direction_id, (shift_x, shift_y) in enumerate(DIRECTIONS):
        row_ids = jnp.broadcast_to(ghost_list[None, :, :, direction_id, :], (4, dom_x, dom_y, ghost_width))
        ghost_piece = jnp.take_along_axis(record, row_ids, axis=3)
        offset = jnp.array([shift_x, shift_y, 0.0, 0.0], jnp.float32)
        ghost_piece = ghost_piece - offset[:, None, None, None]
        arrivals.append(jnp.roll(ghost_piece, (shift_x, shift_y), axis=(1, 2)))
    ghosts = jnp.stack(arrivals, axis=3).reshape(4, dom_x, dom_y, 8 * ghost_width)
    extended = jnp.concatenate([record, ghosts], axis=3)
    ext_flat = jnp.transpose(extended.reshape(4, domains, -1), (1, 0, 2))
    codes_flat = neighbours.reshape(domains, neighbours.shape[2], atom_count)
    counts_flat = counts.reshape(domains, atom_count)

    def forward(inputs):
        extended_one, neighbour_codes, used_slots = inputs
        return short_range(extended_one[:3], extended_one[3], neighbour_codes, used_slots, embedding, radial_weight, product_weight, readout_weight, charge_weight)
    short_energy, charges = lax.map(forward, (ext_flat, codes_flat, counts_flat))
    total_atoms = domains * atom_count
    mean_charge = lax.optimization_barrier(jnp.sum(charges, axis=(0, 2))) / total_atoms
    neutral = charges - mean_charge[None, :, None]
    anchor_x = jnp.broadcast_to(jnp.arange(dom_x)[:, None], (dom_x, dom_y)).reshape(domains).astype(jnp.float32)
    anchor_y = jnp.broadcast_to(jnp.arange(dom_y)[None, :], (dom_x, dom_y)).reshape(domains).astype(jnp.float32)
    anchor = jnp.stack([anchor_x, anchor_y, jnp.zeros((domains,), jnp.float32)], axis=1)
    placed = jnp.transpose(positions.reshape(3, domains, atom_count), (1, 0, 2)) + anchor[:, :, None]
    wave_vectors = wave_table(wave_index, dom_x, dom_y)
    weights = wave_weight(wave_vectors)

    def add_domain(running, inputs):
        spot_coords, amplitude = inputs
        phases = jnp.dot(wave_vectors.T, spot_coords, precision=PRECISE)
        struct_re = running[0] + lax.dot_general(jnp.cos(phases), amplitude, (((1,), (1,)), ((), ())), precision=PRECISE)
        struct_im = running[1] + lax.dot_general(jnp.sin(phases), amplitude, (((1,), (1,)), ((), ())), precision=PRECISE)
        return ((struct_re, struct_im), None)
    zero_block = jnp.zeros((wave_index.shape[1], charges.shape[1]), jnp.float32)
    (struct_re, struct_im), ignored = lax.scan(add_domain, (zero_block, zero_block), (placed, neutral))
    ewald_scale = 1.0 / math.sqrt(total_atoms)
    part_re = (ewald_scale * weights)[:, None] * struct_re
    part_im = (ewald_scale * weights)[:, None] * struct_im

    def backward(inputs):
        extended_one, neighbour_codes, used_slots, spot_coords, amplitude = inputs
        phases = jnp.dot(wave_vectors.T, spot_coords, precision=PRECISE)
        cosine = jnp.cos(phases)
        sine_part = jnp.sin(phases)
        contract = (((0,), (0,)), ((), ()))
        potential = lax.dot_general(part_re, cosine, contract, precision=PRECISE) + lax.dot_general(part_im, sine_part, contract, precision=PRECISE)
        proj_re = jnp.dot(part_re, amplitude, precision=PRECISE)
        proj_im = jnp.dot(part_im, amplitude, precision=PRECISE)
        pulled = jnp.dot(wave_vectors, cosine * proj_im - sine_part * proj_re, precision=PRECISE)

        def local_terms(points):
            return short_range(points, extended_one[3], neighbour_codes, used_slots, embedding, radial_weight, product_weight, readout_weight, charge_weight)
        results, pullback = jax.vjp(local_terms, extended_one[:3])
        ext_grad = pullback((jnp.ones_like(results[0]), potential))[0]
        energy = results[0] + 0.5 * lax.optimization_barrier(jnp.sum(amplitude * potential, axis=0))
        return (energy, ext_grad, pulled)
    energies, ext_grads, pulls = lax.map(backward, (ext_flat, codes_flat, counts_flat, placed, neutral))
    gradients = ext_grads.reshape(dom_x, dom_y, 3, -1)

    def scatter_one(row_ids, values):
        return jnp.zeros((3, atom_count), values.dtype).at[:, row_ids].add(values)
    scatter_all = jax.vmap(jax.vmap(scatter_one))
    returned = jnp.zeros((dom_x, dom_y, 3, atom_count), jnp.float32)
    for direction_id, (shift_x, shift_y) in enumerate(DIRECTIONS):
        begin = atom_count + direction_id * ghost_width
        values = gradients[:, :, :, begin:begin + ghost_width]
        values = jnp.roll(values, (-shift_x, -shift_y), axis=(0, 1))
        returned = returned + scatter_all(ghost_list[:, :, direction_id, :], values)
    total_grad = gradients[:, :, :, :atom_count] + returned + pulls.reshape(dom_x, dom_y, 3, atom_count)
    forces = -jnp.transpose(total_grad, (2, 0, 1, 3))
    return (forces, energies.reshape(dom_x, dom_y, atom_count))
```

```python
import functools
import math

import jax
import jax.numpy as jnp
import numpy as np
from jax import lax
from jax.experimental import pallas as pl
from jax.experimental.pallas import tpu as pltpu
from jax.sharding import PartitionSpec as P

DIRECTIONS = ((-1, -1), (-1, 0), (-1, 1), (0, -1), (0, 1), (1, -1), (1, 0), (1, 1))
SOFTENING = 0.01
BASIS_WIDTH = 2.0
BASIS_STEP = 0.35
SCREENING = 0.02
SLAB_HEIGHT = 2.0
PRECISE = lax.Precision.HIGHEST
MESH = pl.DeviceIdType.MESH
LANES = 128
SUBLANES = 8
VMEM_LIMIT = 40 * 1024 * 1024
F32 = jnp.float32
BF16 = jnp.bfloat16
VMEM = pltpu.VMEM


def half_turn_series(odd, terms):
    nodes = 0.125 * (1.0 + np.cos(np.pi * (np.arange(64) + 0.5) / 64))
    root = np.sqrt(nodes)
    values = np.sin(np.pi * root) / root if odd else np.cos(np.pi * root)
    series = np.polynomial.chebyshev.Chebyshev.fit(nodes, values, terms - 1, domain=[0.0, 0.25])
    return [float(c) for c in series.convert(kind=np.polynomial.Polynomial).coef]


SIN_SERIES = half_turn_series(True, 6)
COS_SERIES = half_turn_series(False, 6)


def horner(series, square):
    total = jnp.full_like(square, series[-1])
    for coefficient in reversed(series[:-1]):
        total = total * square + coefficient
    return total


def cos_sin_turns(turns):
    reduced = turns - jnp.round(turns)
    square = reduced * reduced
    half_sin = reduced * horner(SIN_SERIES, square)
    half_cos = horner(COS_SERIES, square)
    return 1.0 - 2.0 * (half_sin * half_sin), 2.0 * (half_sin * half_cos)


def dot_nn(a, b):
    return lax.dot_general(
        a, b, (((1,), (0,)), ((), ())), precision=PRECISE, preferred_element_type=F32
    )


def dot_tn(a, b):
    return lax.dot_general(
        a, b, (((0,), (0,)), ((), ())), precision=PRECISE, preferred_element_type=F32
    )


def split_bf16(value):
    high = value.astype(BF16)
    return high, (value - high.astype(F32)).astype(BF16)


def dot3(a, b, dims):
    a_high, a_low = split_bf16(a)
    b_high, b_low = split_bf16(b)
    dot = functools.partial(
        lax.dot_general, dimension_numbers=(dims, ((), ())), preferred_element_type=F32
    )
    return dot(a_high, b_high) + (dot(a_high, b_low) + dot(a_low, b_high))


def lookup(table_row, codes):
    rows = codes.shape[0]
    pieces = []
    for part in range(codes.shape[1] // LANES):
        code = codes[:, part * LANES : (part + 1) * LANES]
        low, high = code % LANES, code // LANES
        found = jnp.zeros((rows, LANES), F32)
        for chunk in range(table_row.shape[1] // LANES):
            table = jnp.broadcast_to(
                table_row[:, chunk * LANES : (chunk + 1) * LANES], (rows, LANES)
            )
            picked = jnp.take_along_axis(table, low, axis=1)
            found = jnp.where(high == chunk, picked, found)
        pieces.append(found)
    return jnp.concatenate(pieces, axis=1)


def pick_kernel(record_ref, rows_ref, out_ref):
    rows = rows_ref[...]
    for field in range(4):
        found = lookup(record_ref[field : field + 1, :], rows)
        for direction, shift in enumerate(DIRECTIONS):
            offset = float(shift[field]) if field < 2 else 0.0
            out_ref[direction, field : field + 1, :] = found[direction : direction + 1] - offset
    for direction in range(len(DIRECTIONS)):
        out_ref[direction, 4:, :] = jnp.zeros((4, rows.shape[1]), F32)


def swap_kernel(sign, nx, ny, in_ref, out_ref, send_sem, recv_sem):
    gx, gy = lax.axis_index("gx"), lax.axis_index("gy")
    targets = [
        {
            "gx": lax.rem(gx + sign * sx + nx, nx),
            "gy": lax.rem(gy + sign * sy + ny, ny),
        }
        for sx, sy in DIRECTIONS
    ]
    barrier = pltpu.get_barrier_semaphore()
    for target in targets:
        pl.semaphore_signal(barrier, inc=1, device_id=target, device_id_type=MESH)
    pl.semaphore_wait(barrier, len(targets))
    copies = [
        pltpu.make_async_remote_copy(
            src_ref=in_ref.at[d],
            dst_ref=out_ref.at[d],
            send_sem=send_sem.at[d],
            recv_sem=recv_sem.at[d],
            device_id=target,
            device_id_type=MESH,
        )
        for d, target in enumerate(targets)
    ]
    for copy in copies:
        copy.start()
    for copy in copies:
        copy.wait()


def swap_blocks(blocks, sign, nx, ny, collective_id):
    count = blocks.shape[0]
    return pl.pallas_call(
        functools.partial(swap_kernel, sign, nx, ny),
        name="ghosts_out" if sign == 1 else "ghosts_back",
        out_shape=jax.ShapeDtypeStruct(blocks.shape, F32),
        in_specs=[pl.BlockSpec(memory_space=VMEM)],
        out_specs=pl.BlockSpec(memory_space=VMEM),
        scratch_shapes=[pltpu.SemaphoreType.DMA((count,)), pltpu.SemaphoreType.DMA((count,))],
        compiler_params=pltpu.CompilerParams(collective_id=collective_id, has_side_effects=True),
    )(blocks)


def gather_kernel(nx, ny, in_ref, out_ref, own_sem, line_sem, cross_sem, pair_sem, recv_sem):
    gx, gy = lax.axis_index("gx"), lax.axis_index("gy")
    chips = ny // 2
    core = lax.rem(gy, 2)
    chip = gy // 2
    peer = chip * 2 + (1 - core)
    order = sorted(range(1, nx), key=lambda step: min(step, nx - step))
    lines = [lax.rem(gx + step, nx) for step in order]
    crosses = [lax.rem(chip + step, chips) * 2 + core for step in range(1, chips)]
    partners = [{"gx": x} for x in lines] + [{"gy": y} for y in crosses] + [{"gy": peer}]
    barrier = pltpu.get_barrier_semaphore()
    for partner in partners:
        pl.semaphore_signal(barrier, inc=1, device_id=partner, device_id_type=MESH)
    pl.semaphore_wait(barrier, len(partners))

    def remote(source, slot_x, slot_y, send, device):
        return pltpu.make_async_remote_copy(
            src_ref=source,
            dst_ref=out_ref.at[slot_x, slot_y],
            send_sem=send,
            recv_sem=recv_sem.at[slot_x, slot_y],
            device_id=device,
            device_id_type=MESH,
        )

    def arrived(slot_x, slot_y):
        remote(
            out_ref.at[slot_x, slot_y], slot_x, slot_y, recv_sem.at[slot_x, slot_y], {"gy": peer}
        ).wait_recv()

    sent = []

    def send(source, slot_x, slot_y, semaphore, device):
        copy = remote(source, slot_x, slot_y, semaphore, device)
        copy.start()
        sent.append(copy)

    own = pltpu.make_async_copy(in_ref, out_ref.at[gx, gy], own_sem)
    for index, x in enumerate(lines):
        send(in_ref, gx, gy, line_sem.at[index], {"gx": x})
    for index, y in enumerate(crosses):
        send(in_ref, gx, gy, cross_sem.at[0, index], {"gy": y})
    send(in_ref, gx, gy, pair_sem.at[0, 0], {"gy": peer})
    own.start()
    for row, x in enumerate(lines):
        arrived(x, gy)
        for index, y in enumerate(crosses):
            send(out_ref.at[x, gy], x, gy, cross_sem.at[row + 1, index], {"gy": y})
        send(out_ref.at[x, gy], x, gy, pair_sem.at[row + 1, 0], {"gy": peer})
    for row, x in enumerate([gx] + lines):
        for index, y in enumerate(crosses):
            arrived(x, y)
            send(out_ref.at[x, y], x, y, pair_sem.at[row, index + 1], {"gy": peer})
    for x in [gx] + lines:
        for step in range(chips):
            arrived(x, lax.rem(chip + step, chips) * 2 + (1 - core))
    own.wait()
    for copy in sent:
        copy.wait_send()


def gather_blocks(block, nx, ny, collective_id, name):
    chips = ny // 2
    return pl.pallas_call(
        functools.partial(gather_kernel, nx, ny),
        name=name,
        out_shape=jax.ShapeDtypeStruct((nx, ny) + block.shape, F32),
        in_specs=[pl.BlockSpec(memory_space=VMEM)],
        out_specs=pl.BlockSpec(memory_space=VMEM),
        scratch_shapes=[
            pltpu.SemaphoreType.DMA,
            pltpu.SemaphoreType.DMA((nx - 1,)),
            pltpu.SemaphoreType.DMA((nx, max(chips - 1, 1))),
            pltpu.SemaphoreType.DMA((nx, chips)),
            pltpu.SemaphoreType.DMA((nx, ny)),
        ],
        compiler_params=pltpu.CompilerParams(
            collective_id=collective_id, has_side_effects=True, vmem_limit_bytes=VMEM_LIMIT
        ),
    )(block)


def mixing_of(radial_weight, embedding):
    return jnp.concatenate(
        [radial_weight[b : b + 1, :] * embedding for b in range(radial_weight.shape[0])], axis=0
    )


def short_kernel(
    record_ref, ghost_ref, codes_ref, counts_ref, anchor_ref,
    emb_ref, rw_ref, pw_ref, ro_ref, cw_ref,
    block_ref, energy_ref, geo_ref, gd_ref, gp_ref,
    terms_ref, moments_ref,
):
    slots, atoms = codes_ref.shape
    species, channels = emb_ref.shape
    basis = rw_ref.shape[0]
    codes = codes_ref[...]
    near = []
    for field in range(4):
        row = jnp.concatenate(
            [record_ref[field : field + 1, :]]
            + [ghost_ref[d, field : field + 1, :] for d in range(ghost_ref.shape[0])],
            axis=1,
        )
        near.append(lookup(row, codes))
    separation = [near[x] - record_ref[x : x + 1, :] for x in range(3)]
    square = separation[0] * separation[0]
    square = square + separation[1] * separation[1] + separation[2] * separation[2]
    radius = jnp.sqrt(square + SOFTENING)
    inverse = 1.0 / radius
    kind = near[3]
    slot = lax.broadcasted_iota(jnp.int32, (slots, atoms), 0)
    live = jnp.where(slot < counts_ref[...], 1.0, 0.0)
    unit = [part * inverse for part in separation]
    for x in range(3):
        geo_ref[x] = unit[x]
    geo_ref[3] = radius
    geo_ref[4] = kind
    for b in range(basis):
        offset = radius - BASIS_STEP * b
        radial = jnp.exp(-BASIS_WIDTH * (offset * offset)) * live
        terms_ref[b] = radial
        for x in range(3):
            terms_ref[(x + 1) * basis + b] = unit[x] * radial

    def reduce_term(q, carry):
        term = terms_ref[q]
        near_kind = geo_ref[4]
        rows = [
            jnp.sum(jnp.where(near_kind == float(s), term, 0.0), axis=0, keepdims=True)
            for s in range(species)
        ]
        moments_ref[q] = jnp.concatenate(rows, axis=0)
        return carry

    lax.fori_loop(0, 4 * basis, reduce_term, 0, unroll=2)
    mixing = mixing_of(rw_ref[...], emb_ref[...])
    norm = 1.0 / math.sqrt(slots)
    moments = [
        moments_ref[q * basis : (q + 1) * basis].reshape(basis * species, atoms) for q in range(4)
    ]
    own_species = lax.broadcasted_iota(jnp.int32, (species, atoms), 0).astype(F32)
    onehot = jnp.where(own_species == record_ref[3:4, :], 1.0, 0.0)
    scalar = norm * dot_tn(mixing, moments[0]) + dot_tn(emb_ref[...], onehot)
    vectorial = [norm * dot_tn(mixing, moments[x + 1]) for x in range(3)]
    squares = vectorial[0] * vectorial[0] + vectorial[1] * vectorial[1] + vectorial[2] * vectorial[2]
    invariants = jnp.concatenate([scalar, squares], axis=0)
    before = dot_tn(pw_ref[...], invariants)
    gate = 1.0 / (1.0 + jnp.exp(-before))
    hidden = before * gate
    energy_ref[...] = jnp.sum(hidden * ro_ref[...], axis=0, keepdims=True)
    block_ref[:channels, :] = dot_tn(cw_ref[...], scalar)
    block_ref[channels : channels + 3, :] = record_ref[:3, :] + anchor_ref[...]
    block_ref[channels + 3 :, :] = jnp.zeros((SUBLANES - 3, atoms), F32)
    slope = ro_ref[...] * (gate + hidden * (1.0 - gate))
    back = dot_nn(pw_ref[...], slope)
    gd_ref[...] = norm * dot_nn(mixing, back[:channels])
    for x in range(3):
        grad = norm * dot_nn(mixing, 2.0 * vectorial[x] * back[channels:])
        gp_ref[x * basis : (x + 1) * basis] = grad.reshape(basis, species, atoms)


def structure_kernel(neutralise, total, channels, spans, blocks_ref, cols_ref, rows_ref, out_ref, mean_ref):
    domains = blocks_ref.shape[0]
    wave_blocks = out_ref.shape[0]
    atoms = blocks_ref.shape[2]
    if neutralise:
        summed = blocks_ref[0, :channels, :]
        for d in range(1, domains):
            summed = summed + blocks_ref[d, :channels, :]
        mean = jnp.sum(summed, axis=1, keepdims=True) / total
    else:
        mean = jnp.zeros((channels, 1), F32)
    mean_ref[...] = jnp.broadcast_to(mean, mean_ref.shape)

    def one_block(w, carry):
        cols = cols_ref[pl.ds(pl.multiple_of(w * LANES, LANES), LANES), :]

        def add_domain(d, running):
            block = blocks_ref[d]
            turns = cols[:, 0:1] * (block[channels : channels + 1] * (1.0 / spans[0]))
            turns = turns + cols[:, 1:2] * (block[channels + 1 : channels + 2] * (1.0 / spans[1]))
            turns = turns + cols[:, 2:3] * (block[channels + 2 : channels + 3] * (1.0 / spans[2]))
            cosine, sine = cos_sin_turns(turns)
            waves = jnp.concatenate([cosine, sine], axis=0)
            return running + dot3(block[:channels] - mean, waves, ((1,), (1,)))

        summed = lax.fori_loop(0, domains, add_domain, jnp.zeros((channels, 2 * LANES), F32))
        rows = rows_ref[w]
        squared = jnp.zeros((1, LANES), F32)
        for x in range(3):
            wave = rows[x : x + 1] * (2.0 * math.pi / spans[x])
            squared = squared + wave * wave
        weight = jnp.exp(-0.5 * SCREENING * SCREENING * squared) / (squared + 1.0)
        weight = weight * (1.0 / math.sqrt(total))
        out_ref[w] = summed * jnp.concatenate([weight, weight], axis=1)
        return carry

    lax.fori_loop(0, wave_blocks, one_block, 0)


def back_kernel(
    spans, struct_ref, cols_ref, rows_ref, block_ref, mean_ref, short_ref, geo_ref, codes_ref,
    counts_ref, gd_ref, gp_ref, rw_ref, emb_ref, cw_ref,
    energy_ref, own_ref, ghost_ref,
    gd_rows_ref, pair_ref, acc_ref,
):
    slots, atoms = codes_ref.shape
    species, channels = emb_ref.shape
    basis = rw_ref.shape[0]
    wave_blocks = struct_ref.shape[0]
    neutral = block_ref[:channels, :] - mean_ref[:, 0:1]
    neutral_high, neutral_low = split_bf16(neutral)
    scaled = [block_ref[channels + x : channels + x + 1, :] * (1.0 / spans[x]) for x in range(3)]
    over_rows = ((0,), (0,))

    def add_waves(w, carry):
        potential, pulled = carry
        cols = cols_ref[pl.ds(pl.multiple_of(w * LANES, LANES), LANES), :]
        turns = cols[:, 0:1] * scaled[0] + cols[:, 1:2] * scaled[1] + cols[:, 2:3] * scaled[2]
        cosine, sine = cos_sin_turns(turns)
        waves = jnp.concatenate([cosine, sine], axis=0)
        struct = struct_ref[w]
        potential = potential + dot3(struct, waves, ((1,), (0,)))
        high, low = split_bf16(struct)
        dot = functools.partial(
            lax.dot_general, dimension_numbers=(over_rows, ((), ())), preferred_element_type=F32
        )
        projected = dot(high, neutral_high) + (dot(high, neutral_low) + dot(low, neutral_high))
        torque = cosine * projected[LANES:] - sine * projected[:LANES]
        return potential, pulled + dot3(rows_ref[w], torque, ((1,), (0,)))

    potential, pulled = lax.fori_loop(
        0,
        wave_blocks,
        add_waves,
        (jnp.zeros((channels, atoms), F32), jnp.zeros((SUBLANES, atoms), F32)),
    )
    energy_ref[...] = short_ref[...] + 0.5 * jnp.sum(neutral * potential, axis=0, keepdims=True)
    mixing = mixing_of(rw_ref[...], emb_ref[...])
    norm = 1.0 / math.sqrt(slots)
    density_grad = gd_ref[...] + norm * dot_nn(mixing, dot_nn(cw_ref[...], potential))
    gd_rows_ref[...] = density_grad.reshape(basis, species, atoms)

    def pair_rows(i, carry):
        start = pl.multiple_of(i * SUBLANES, SUBLANES)
        window = pl.ds(start, SUBLANES)
        unit = [geo_ref[x, window, :] for x in range(3)]
        radius = geo_ref[3, window, :]
        kind = geo_ref[4, window, :]
        masks = [kind == float(s) for s in range(1, species)]
        slot = lax.broadcasted_iota(jnp.int32, (SUBLANES, atoms), 0) + start
        live = jnp.where(slot < counts_ref[...], 1.0, 0.0)

        def of_kind(table):
            chosen = jnp.broadcast_to(table[0:1, :], (SUBLANES, atoms))
            for s in range(1, species):
                chosen = jnp.where(masks[s - 1], table[s : s + 1, :], chosen)
            return chosen

        along = jnp.zeros((SUBLANES, atoms), F32)
        turn = [jnp.zeros((SUBLANES, atoms), F32) for x in range(3)]
        for b in range(basis):
            offset = radius - BASIS_STEP * b
            radial = jnp.exp(-BASIS_WIDTH * (offset * offset)) * live
            total = of_kind(gd_rows_ref[b])
            for x in range(3):
                polar = of_kind(gp_ref[x * basis + b])
                total = total + unit[x] * polar
                turn[x] = turn[x] + radial * polar
            along = along + (-2.0 * BASIS_WIDTH) * offset * radial * total
        inverse = 1.0 / radius
        swing = turn[0] * unit[0] + turn[1] * unit[1] + turn[2] * unit[2]
        radial_part = along - swing * inverse
        for x in range(3):
            pair_ref[x, window, :] = unit[x] * radial_part + turn[x] * inverse
        return carry

    lax.fori_loop(0, slots // SUBLANES, pair_rows, 0)
    chunks = acc_ref.shape[0] // 6
    acc_ref[...] = jnp.zeros(acc_ref.shape, F32)
    group = 4

    def scatter_rows(i, carry):
        start = i * group
        total = None
        for k in range(group):
            code = codes_ref[pl.ds(start + k, 1), :]
            low, high = code % LANES, code // LANES
            spots = lax.broadcasted_iota(jnp.int32, (LANES, atoms), 0)
            onehot = jnp.where(spots == low, 1.0, 0.0).astype(BF16)
            chunk_ids = lax.broadcasted_iota(jnp.int32, (chunks, atoms), 0)
            here = chunk_ids == high
            values = jnp.concatenate(
                [jnp.where(here, pair_ref[x, pl.ds(start + k, 1), :], 0.0) for x in range(3)],
                axis=0,
            )
            values = jnp.concatenate(split_bf16(values), axis=0)
            part = lax.dot_general(
                values, onehot, (((1,), (1,)), ((), ())), preferred_element_type=F32
            )
            total = part if total is None else total + part
        acc_ref[...] += total
        return carry

    lax.fori_loop(0, slots // group, scatter_rows, 0)
    summed = acc_ref[: 3 * chunks, :] + acc_ref[3 * chunks :, :]
    own_chunks = atoms // LANES
    own_ref[...] = jnp.zeros(own_ref.shape, F32)
    ghost_ref[...] = jnp.zeros(ghost_ref.shape, F32)
    for x in range(3):
        received = jnp.concatenate(
            [summed[x * chunks + h : x * chunks + h + 1, :] for h in range(own_chunks)], axis=1
        )
        centre = jnp.sum(pair_ref[x], axis=0, keepdims=True)
        wave_pull = pulled[x : x + 1, :] * (2.0 * math.pi / spans[x])
        own_ref[x : x + 1, :] = received - centre + wave_pull
        for d in range(ghost_ref.shape[0]):
            row = x * chunks + own_chunks + d
            ghost_ref[d, x : x + 1, :] = summed[row : row + 1, :]


def owners_kernel(back_ref, rows_ref, own_ref, out_ref):
    atoms = own_ref.shape[1]
    total = own_ref[...]
    for d in range(back_ref.shape[0]):
        spots = lax.broadcasted_iota(jnp.int32, (atoms, rows_ref.shape[1]), 0)
        onehot = jnp.where(spots == rows_ref[d : d + 1, :], 1.0, 0.0).astype(BF16)
        values = jnp.concatenate(split_bf16(back_ref[d]), axis=0)
        part = lax.dot_general(values, onehot, (((1,), (1,)), ((), ())), preferred_element_type=F32)
        total = total + part[:SUBLANES] + part[SUBLANES:]
    out_ref[...] = -total[:3]


def local_call(kernel, name, outs, scratch, *args):
    return pl.pallas_call(
        kernel,
        name=name,
        out_shape=[jax.ShapeDtypeStruct(shape, F32) for shape in outs],
        in_specs=[pl.BlockSpec(memory_space=VMEM)] * len(args),
        out_specs=[pl.BlockSpec(memory_space=VMEM)] * len(outs),
        scratch_shapes=[pltpu.VMEM(shape, F32) for shape in scratch],
        compiler_params=pltpu.CompilerParams(vmem_limit_bytes=VMEM_LIMIT),
    )(*args)


def on_device(
    positions,
    species,
    neighbours,
    counts,
    ghost_list,
    wave_index,
    embedding,
    radial_weight,
    product_weight,
    readout_weight,
    charge_weight,
):
    nx, ny = lax.axis_size("gx"), lax.axis_size("gy")
    domains = nx * ny
    atoms = positions.shape[3]
    codes = neighbours[0, 0]
    slots = codes.shape[0]
    used = counts[0]
    ghost_rows = ghost_list[0, 0]
    directions, width = ghost_rows.shape
    waves = wave_index.shape[1]
    kinds, channels = embedding.shape
    basis = radial_weight.shape[0]
    spans = (float(nx), float(ny), SLAB_HEIGHT)
    total_atoms = float(atoms * domains)
    gx, gy = lax.axis_index("gx"), lax.axis_index("gy")
    record = jnp.concatenate(
        [positions.reshape(3, atoms), species[0].astype(F32)], axis=0
    )
    anchor = jnp.stack([gx.astype(F32), gy.astype(F32), jnp.zeros((), F32)]).reshape(3, 1)
    wave_float = wave_index.astype(F32)
    wave_cols = wave_float.T
    wave_rows = jnp.pad(
        wave_float.reshape(3, waves // LANES, LANES).transpose(1, 0, 2), ((0, 0), (0, 5), (0, 0))
    )
    readout = readout_weight.reshape(channels, 1)

    (outgoing,) = local_call(
        pick_kernel, "pick_ghosts", [(directions, SUBLANES, width)], [], record, ghost_rows
    )
    ghosts = swap_blocks(outgoing, 1, nx, ny, 0)
    block, short_energy, geometry, density_grad, polar_grad = local_call(
        short_kernel,
        "short_range",
        [
            (channels + SUBLANES, atoms),
            (1, atoms),
            (5, slots, atoms),
            (basis * kinds, atoms),
            (3 * basis, kinds, atoms),
        ],
        [(4 * basis, slots, atoms), (4 * basis, kinds, atoms)],
        record, ghosts, codes, used, anchor,
        embedding, radial_weight, product_weight, readout, charge_weight,
    )
    wave_blocks = waves // LANES
    if wave_blocks == domains:
        mine = gx * ny + gy
        blocks = gather_blocks(block, nx, ny, 1, "gather_charges")
        struct, mean = local_call(
            functools.partial(structure_kernel, True, total_atoms, channels, spans),
            "structure",
            [(1, channels, 2 * LANES), (channels, LANES)],
            [],
            blocks.reshape(domains, channels + SUBLANES, atoms),
            lax.dynamic_slice_in_dim(wave_cols, mine * LANES, LANES, axis=0),
            lax.dynamic_slice_in_dim(wave_rows, mine, 1, axis=0),
        )
        struct = gather_blocks(struct[0], nx, ny, 2, "gather_structure")
        struct = struct.reshape(wave_blocks, channels, 2 * LANES)
    else:
        charge_total = lax.psum(jnp.sum(block[:channels], axis=1, keepdims=True), ("gx", "gy"))
        mean = jnp.broadcast_to(charge_total / total_atoms, (channels, LANES))
        neutral = jnp.concatenate([block[:channels] - mean[:, :1], block[channels:]], axis=0)
        struct, unused = local_call(
            functools.partial(structure_kernel, False, total_atoms, channels, spans),
            "structure",
            [(wave_blocks, channels, 2 * LANES), (channels, LANES)],
            [],
            neutral[None],
            wave_cols,
            wave_rows,
        )
        struct = lax.psum(struct, ("gx", "gy"))
    chunks = 16 * -(-(atoms // LANES + directions * width // LANES) // 16)
    energy, own_grad, ghost_grad = local_call(
        functools.partial(back_kernel, spans),
        "gradients",
        [(1, atoms), (SUBLANES, atoms), (directions, SUBLANES, width)],
        [(basis, kinds, atoms), (3, slots, atoms), (6 * chunks, LANES)],
        struct, wave_cols, wave_rows, block, mean, short_energy, geometry, codes, used,
        density_grad, polar_grad, radial_weight, embedding, charge_weight,
    )
    back = swap_blocks(ghost_grad, -1, nx, ny, 3)
    (forces,) = local_call(owners_kernel, "owners", [(3, atoms)], [], back, ghost_rows, own_grad)
    return (forces[:, None, None, :], energy[None])


def solution(mesh):
    in_specs = (
        P(None, ("group", "gx"), "gy", None),
        P(("group", "gx"), "gy", None),
        P(("group", "gx"), "gy", None, None),
        P(("group", "gx"), "gy", None),
        P(("group", "gx"), "gy", None, None),
        P(),
        P(),
        P(),
        P(),
        P(),
        P(),
    )
    out_specs = (P(None, ("group", "gx"), "gy", None), P(("group", "gx"), "gy", None))
    return jax.shard_map(
        on_device, mesh=mesh, in_specs=in_specs, out_specs=out_specs, check_vma=False
    )
```

```python
import functools
import math

import jax
import jax.numpy as jnp
import numpy as np
from jax import lax
from jax.experimental import pallas as pl
from jax.experimental.pallas import tpu as pltpu
from jax.sharding import PartitionSpec as P

DIRECTIONS = ((-1, -1), (-1, 0), (-1, 1), (0, -1), (0, 1), (1, -1), (1, 0), (1, 1))
SOFTENING = 0.01
BASIS_WIDTH = 2.0
BASIS_STEP = 0.35
SCREENING = 0.02
SLAB_HEIGHT = 2.0
PRECISE = lax.Precision.HIGHEST
MESH = pl.DeviceIdType.MESH
LANES = 128
SUBLANES = 8
VMEM_LIMIT = 40 * 1024 * 1024
F32 = jnp.float32
BF16 = jnp.bfloat16
VMEM = pltpu.VMEM


def half_turn_series(odd, terms):
    nodes = 0.125 * (1.0 + np.cos(np.pi * (np.arange(64) + 0.5) / 64))
    root = np.sqrt(nodes)
    values = np.sin(np.pi * root) / root if odd else np.cos(np.pi * root)
    series = np.polynomial.chebyshev.Chebyshev.fit(nodes, values, terms - 1, domain=[0.0, 0.25])
    return [float(c) for c in series.convert(kind=np.polynomial.Polynomial).coef]


SIN_SERIES = half_turn_series(True, 6)
COS_SERIES = half_turn_series(False, 6)


def horner(series, square):
    total = jnp.full_like(square, series[-1])
    for coefficient in reversed(series[:-1]):
        total = total * square + coefficient
    return total


def cos_sin_turns(turns):
    reduced = turns - jnp.round(turns)
    square = reduced * reduced
    half_sin = reduced * horner(SIN_SERIES, square)
    half_cos = horner(COS_SERIES, square)
    return 1.0 - 2.0 * (half_sin * half_sin), 2.0 * (half_sin * half_cos)


def dot_nn(a, b):
    return lax.dot_general(
        a, b, (((1,), (0,)), ((), ())), precision=PRECISE, preferred_element_type=F32
    )


def dot_tn(a, b):
    return lax.dot_general(
        a, b, (((0,), (0,)), ((), ())), precision=PRECISE, preferred_element_type=F32
    )


def split_bf16(value):
    high = value.astype(BF16)
    return high, (value - high.astype(F32)).astype(BF16)


def dot3(a, b, dims):
    a_high, a_low = split_bf16(a)
    b_high, b_low = split_bf16(b)
    dot = functools.partial(
        lax.dot_general, dimension_numbers=(dims, ((), ())), preferred_element_type=F32
    )
    return dot(a_high, b_high) + (dot(a_high, b_low) + dot(a_low, b_high))


def lookup(table_row, codes):
    rows = codes.shape[0]
    pieces = []
    for part in range(codes.shape[1] // LANES):
        code = codes[:, part * LANES : (part + 1) * LANES]
        low, high = code % LANES, code // LANES
        found = jnp.zeros((rows, LANES), F32)
        for chunk in range(table_row.shape[1] // LANES):
            table = jnp.broadcast_to(
                table_row[:, chunk * LANES : (chunk + 1) * LANES], (rows, LANES)
            )
            picked = jnp.take_along_axis(table, low, axis=1)
            found = jnp.where(high == chunk, picked, found)
        pieces.append(found)
    return jnp.concatenate(pieces, axis=1)


def pick_kernel(record_ref, rows_ref, out_ref):
    rows = rows_ref[...]
    for field in range(4):
        found = lookup(record_ref[field : field + 1, :], rows)
        for direction, shift in enumerate(DIRECTIONS):
            offset = float(shift[field]) if field < 2 else 0.0
            out_ref[direction, field : field + 1, :] = found[direction : direction + 1] - offset
    for direction in range(len(DIRECTIONS)):
        out_ref[direction, 4:, :] = jnp.zeros((4, rows.shape[1]), F32)


def swap_kernel(sign, nx, ny, in_ref, out_ref, send_sem, recv_sem):
    gx, gy = lax.axis_index("gx"), lax.axis_index("gy")
    targets = [
        {
            "gx": lax.rem(gx + sign * sx + nx, nx),
            "gy": lax.rem(gy + sign * sy + ny, ny),
        }
        for sx, sy in DIRECTIONS
    ]
    barrier = pltpu.get_barrier_semaphore()
    for target in targets:
        pl.semaphore_signal(barrier, inc=1, device_id=target, device_id_type=MESH)
    pl.semaphore_wait(barrier, len(targets))
    copies = [
        pltpu.make_async_remote_copy(
            src_ref=in_ref.at[d],
            dst_ref=out_ref.at[d],
            send_sem=send_sem.at[d],
            recv_sem=recv_sem.at[d],
            device_id=target,
            device_id_type=MESH,
        )
        for d, target in enumerate(targets)
    ]
    for copy in copies:
        copy.start()
    for copy in copies:
        copy.wait()


def swap_blocks(blocks, sign, nx, ny, collective_id):
    count = blocks.shape[0]
    return pl.pallas_call(
        functools.partial(swap_kernel, sign, nx, ny),
        name="ghosts_out" if sign == 1 else "ghosts_back",
        out_shape=jax.ShapeDtypeStruct(blocks.shape, F32),
        in_specs=[pl.BlockSpec(memory_space=VMEM)],
        out_specs=pl.BlockSpec(memory_space=VMEM),
        scratch_shapes=[pltpu.SemaphoreType.DMA((count,)), pltpu.SemaphoreType.DMA((count,))],
        compiler_params=pltpu.CompilerParams(collective_id=collective_id, has_side_effects=True),
    )(blocks)


def mixing_of(radial_weight, embedding):
    return jnp.concatenate(
        [radial_weight[b : b + 1, :] * embedding for b in range(radial_weight.shape[0])], axis=0
    )


def short_kernel(
    record_ref, ghost_ref, codes_ref, counts_ref, anchor_ref,
    emb_ref, rw_ref, pw_ref, ro_ref, cw_ref,
    block_ref, energy_ref, geo_ref, gd_ref, gp_ref,
    terms_ref, moments_ref,
):
    slots, atoms = codes_ref.shape
    species, channels = emb_ref.shape
    basis = rw_ref.shape[0]
    codes = codes_ref[...]
    near = []
    for field in range(4):
        row = jnp.concatenate(
            [record_ref[field : field + 1, :]]
            + [ghost_ref[d, field : field + 1, :] for d in range(ghost_ref.shape[0])],
            axis=1,
        )
        near.append(lookup(row, codes))
    separation = [near[x] - record_ref[x : x + 1, :] for x in range(3)]
    square = separation[0] * separation[0]
    square = square + separation[1] * separation[1] + separation[2] * separation[2]
    radius = jnp.sqrt(square + SOFTENING)
    inverse = 1.0 / radius
    kind = near[3]
    slot = lax.broadcasted_iota(jnp.int32, (slots, atoms), 0)
    live = jnp.where(slot < counts_ref[...], 1.0, 0.0)
    unit = [part * inverse for part in separation]
    for x in range(3):
        geo_ref[x] = unit[x]
    geo_ref[3] = radius
    geo_ref[4] = kind
    for b in range(basis):
        offset = radius - BASIS_STEP * b
        radial = jnp.exp(-BASIS_WIDTH * (offset * offset)) * live
        terms_ref[b] = radial
        for x in range(3):
            terms_ref[(x + 1) * basis + b] = unit[x] * radial

    def reduce_term(q, carry):
        term = terms_ref[q]
        near_kind = geo_ref[4]
        rows = [
            jnp.sum(jnp.where(near_kind == float(s), term, 0.0), axis=0, keepdims=True)
            for s in range(species)
        ]
        moments_ref[q] = jnp.concatenate(rows, axis=0)
        return carry

    lax.fori_loop(0, 4 * basis, reduce_term, 0, unroll=2)
    mixing = mixing_of(rw_ref[...], emb_ref[...])
    norm = 1.0 / math.sqrt(slots)
    moments = [
        moments_ref[q * basis : (q + 1) * basis].reshape(basis * species, atoms) for q in range(4)
    ]
    own_species = lax.broadcasted_iota(jnp.int32, (species, atoms), 0).astype(F32)
    onehot = jnp.where(own_species == record_ref[3:4, :], 1.0, 0.0)
    scalar = norm * dot_tn(mixing, moments[0]) + dot_tn(emb_ref[...], onehot)
    vectorial = [norm * dot_tn(mixing, moments[x + 1]) for x in range(3)]
    squares = vectorial[0] * vectorial[0] + vectorial[1] * vectorial[1] + vectorial[2] * vectorial[2]
    invariants = jnp.concatenate([scalar, squares], axis=0)
    before = dot_tn(pw_ref[...], invariants)
    gate = 1.0 / (1.0 + jnp.exp(-before))
    hidden = before * gate
    energy_ref[...] = jnp.sum(hidden * ro_ref[...], axis=0, keepdims=True)
    block_ref[:channels, :] = dot_tn(cw_ref[...], scalar)
    block_ref[channels : channels + 3, :] = record_ref[:3, :] + anchor_ref[...]
    block_ref[channels + 3 :, :] = jnp.zeros((SUBLANES - 3, atoms), F32)
    slope = ro_ref[...] * (gate + hidden * (1.0 - gate))
    back = dot_nn(pw_ref[...], slope)
    gd_ref[...] = norm * dot_nn(mixing, back[:channels])
    for x in range(3):
        grad = norm * dot_nn(mixing, 2.0 * vectorial[x] * back[channels:])
        gp_ref[x * basis : (x + 1) * basis] = grad.reshape(basis, species, atoms)


def structure_kernel(total, channels, spans, block_ref, cols_ref, rows_ref, out_ref):
    def one_block(w, carry):
        cols = cols_ref[pl.ds(pl.multiple_of(w * LANES, LANES), LANES), :]
        turns = jnp.zeros((LANES, block_ref.shape[1]), F32)
        for x in range(3):
            placed = block_ref[channels + x : channels + x + 1, :]
            turns = turns + cols[:, x : x + 1] * (placed * (1.0 / spans[x]))
        waves = jnp.concatenate(cos_sin_turns(turns), axis=0)
        rows = rows_ref[w]
        squared = jnp.zeros((1, LANES), F32)
        for x in range(3):
            wave = rows[x : x + 1] * (2.0 * math.pi / spans[x])
            squared = squared + wave * wave
        weight = jnp.exp(-0.5 * SCREENING * SCREENING * squared) / (squared + 1.0)
        weight = weight * (1.0 / math.sqrt(total))
        factors = dot3(block_ref[:channels, :], waves, ((1,), (1,)))
        out_ref[w] = factors * jnp.concatenate([weight, weight], axis=1)
        return carry

    lax.fori_loop(0, out_ref.shape[0], one_block, 0)


def back_kernel(
    spans, struct_ref, cols_ref, rows_ref, block_ref, mean_ref, short_ref, geo_ref, codes_ref,
    counts_ref, gd_ref, gp_ref, rw_ref, emb_ref, cw_ref,
    energy_ref, own_ref, ghost_ref,
    gd_rows_ref, pair_ref, acc_ref,
):
    slots, atoms = codes_ref.shape
    species, channels = emb_ref.shape
    basis = rw_ref.shape[0]
    wave_blocks = struct_ref.shape[0]
    neutral = block_ref[:channels, :] - mean_ref[:, 0:1]
    neutral_high, neutral_low = split_bf16(neutral)
    scaled = [block_ref[channels + x : channels + x + 1, :] * (1.0 / spans[x]) for x in range(3)]
    over_rows = ((0,), (0,))

    def add_waves(w, carry):
        potential, pulled = carry
        cols = cols_ref[pl.ds(pl.multiple_of(w * LANES, LANES), LANES), :]
        turns = cols[:, 0:1] * scaled[0] + cols[:, 1:2] * scaled[1] + cols[:, 2:3] * scaled[2]
        cosine, sine = cos_sin_turns(turns)
        waves = jnp.concatenate([cosine, sine], axis=0)
        struct = struct_ref[w]
        potential = potential + dot3(struct, waves, ((1,), (0,)))
        high, low = split_bf16(struct)
        dot = functools.partial(
            lax.dot_general, dimension_numbers=(over_rows, ((), ())), preferred_element_type=F32
        )
        projected = dot(high, neutral_high) + (dot(high, neutral_low) + dot(low, neutral_high))
        torque = cosine * projected[LANES:] - sine * projected[:LANES]
        return potential, pulled + dot3(rows_ref[w], torque, ((1,), (0,)))

    potential, pulled = lax.fori_loop(
        0,
        wave_blocks,
        add_waves,
        (jnp.zeros((channels, atoms), F32), jnp.zeros((SUBLANES, atoms), F32)),
    )
    energy_ref[...] = short_ref[...] + 0.5 * jnp.sum(neutral * potential, axis=0, keepdims=True)
    mixing = mixing_of(rw_ref[...], emb_ref[...])
    norm = 1.0 / math.sqrt(slots)
    density_grad = gd_ref[...] + norm * dot_nn(mixing, dot_nn(cw_ref[...], potential))
    gd_rows_ref[...] = density_grad.reshape(basis, species, atoms)

    def pair_rows(i, carry):
        start = pl.multiple_of(i * SUBLANES, SUBLANES)
        window = pl.ds(start, SUBLANES)
        unit = [geo_ref[x, window, :] for x in range(3)]
        radius = geo_ref[3, window, :]
        kind = geo_ref[4, window, :]
        masks = [kind == float(s) for s in range(1, species)]
        slot = lax.broadcasted_iota(jnp.int32, (SUBLANES, atoms), 0) + start
        live = jnp.where(slot < counts_ref[...], 1.0, 0.0)

        def of_kind(table):
            chosen = jnp.broadcast_to(table[0:1, :], (SUBLANES, atoms))
            for s in range(1, species):
                chosen = jnp.where(masks[s - 1], table[s : s + 1, :], chosen)
            return chosen

        along = jnp.zeros((SUBLANES, atoms), F32)
        turn = [jnp.zeros((SUBLANES, atoms), F32) for x in range(3)]
        for b in range(basis):
            offset = radius - BASIS_STEP * b
            radial = jnp.exp(-BASIS_WIDTH * (offset * offset)) * live
            total = of_kind(gd_rows_ref[b])
            for x in range(3):
                polar = of_kind(gp_ref[x * basis + b])
                total = total + unit[x] * polar
                turn[x] = turn[x] + radial * polar
            along = along + (-2.0 * BASIS_WIDTH) * offset * radial * total
        inverse = 1.0 / radius
        swing = turn[0] * unit[0] + turn[1] * unit[1] + turn[2] * unit[2]
        radial_part = along - swing * inverse
        for x in range(3):
            pair_ref[x, window, :] = unit[x] * radial_part + turn[x] * inverse
        return carry

    lax.fori_loop(0, slots // SUBLANES, pair_rows, 0)
    chunks = acc_ref.shape[0] // 6
    acc_ref[...] = jnp.zeros(acc_ref.shape, F32)
    group = 4

    def scatter_rows(i, carry):
        start = i * group
        total = None
        for k in range(group):
            code = codes_ref[pl.ds(start + k, 1), :]
            low, high = code % LANES, code // LANES
            spots = lax.broadcasted_iota(jnp.int32, (LANES, atoms), 0)
            onehot = jnp.where(spots == low, 1.0, 0.0).astype(BF16)
            chunk_ids = lax.broadcasted_iota(jnp.int32, (chunks, atoms), 0)
            here = chunk_ids == high
            values = jnp.concatenate(
                [jnp.where(here, pair_ref[x, pl.ds(start + k, 1), :], 0.0) for x in range(3)],
                axis=0,
            )
            values = jnp.concatenate(split_bf16(values), axis=0)
            part = lax.dot_general(
                values, onehot, (((1,), (1,)), ((), ())), preferred_element_type=F32
            )
            total = part if total is None else total + part
        acc_ref[...] += total
        return carry

    lax.fori_loop(0, slots // group, scatter_rows, 0)
    summed = acc_ref[: 3 * chunks, :] + acc_ref[3 * chunks :, :]
    own_chunks = atoms // LANES
    own_ref[...] = jnp.zeros(own_ref.shape, F32)
    ghost_ref[...] = jnp.zeros(ghost_ref.shape, F32)
    for x in range(3):
        received = jnp.concatenate(
            [summed[x * chunks + h : x * chunks + h + 1, :] for h in range(own_chunks)], axis=1
        )
        centre = jnp.sum(pair_ref[x], axis=0, keepdims=True)
        wave_pull = pulled[x : x + 1, :] * (2.0 * math.pi / spans[x])
        own_ref[x : x + 1, :] = received - centre + wave_pull
        for d in range(ghost_ref.shape[0]):
            row = x * chunks + own_chunks + d
            ghost_ref[d, x : x + 1, :] = summed[row : row + 1, :]


def owned(values, rows, atoms):
    ids = lax.broadcasted_iota(jnp.int32, (atoms, rows.shape[1]), 0)
    onehot = jnp.where(ids == rows, 1.0, 0.0).astype(BF16)
    halves = jnp.concatenate(split_bf16(values), axis=0)
    part = lax.dot_general(halves, onehot, (((1,), (1,)), ((), ())), preferred_element_type=F32)
    return part[:SUBLANES] + part[SUBLANES:]


def owners_kernel(back_ref, rows_ref, own_ref, out_ref):
    total = own_ref[...]
    for d in range(back_ref.shape[0]):
        total = total + owned(back_ref[d], rows_ref[d : d + 1, :], own_ref.shape[1])
    out_ref[...] = -total[:3]


class Spread:
    def __init__(self, nx, ny, buffer, line_sem, cross_sem, pair_sem, recv_sem):
        self.gx, self.gy = lax.axis_index("gx"), lax.axis_index("gy")
        self.nx, self.chips = nx, ny // 2
        self.core = lax.rem(self.gy, 2)
        self.chip = self.gy // 2
        self.peer = self.chip * 2 + (1 - self.core)
        order = sorted(range(1, nx), key=lambda step: min(step, nx - step))
        self.lines = [lax.rem(self.gx + step, nx) for step in order]
        self.crosses = [
            lax.rem(self.chip + step, self.chips) * 2 + self.core for step in range(1, self.chips)
        ]
        self.buffer = buffer
        self.line_sem, self.cross_sem, self.pair_sem = line_sem, cross_sem, pair_sem
        self.recv_sem = recv_sem
        self.sent = []

    def remote(self, x, y, send_sem, device):
        return pltpu.make_async_remote_copy(
            src_ref=self.buffer.at[x, y],
            dst_ref=self.buffer.at[x, y],
            send_sem=send_sem,
            recv_sem=self.recv_sem.at[x, y],
            device_id=device,
            device_id_type=MESH,
        )

    def send(self, x, y, send_sem, device):
        copy = self.remote(x, y, send_sem, device)
        copy.start()
        self.sent.append(copy)

    def arrived(self, x, y):
        self.remote(x, y, self.line_sem.at[0], {"gy": self.peer}).wait_recv()

    def to_chip(self, x, row):
        for index, y in enumerate(self.crosses):
            self.send(x, self.gy, self.cross_sem.at[row, index], {"gy": y})
        self.send(x, self.gy, self.pair_sem.at[row, 0], {"gy": self.peer})

    def start(self):
        for index, x in enumerate(self.lines):
            self.send(self.gx, self.gy, self.line_sem.at[index], {"gx": x})
        self.to_chip(self.gx, 0)

    def take_lines(self, beside):
        for row, x in enumerate(self.lines):
            self.arrived(x, self.gy)
            self.to_chip(x, row + 1)
            beside(row, x, self.gy)

    def take_crosses(self, beside):
        for row, x in enumerate([self.gx] + self.lines):
            for index, y in enumerate(self.crosses):
                self.arrived(x, y)
                self.send(x, y, self.pair_sem.at[row, index + 1], {"gy": self.peer})
                beside(row, x, y)

    def take_pairs(self, beside, carry):
        def one(j, running):
            x = lax.rem(self.gx + j // self.chips, self.nx)
            y = lax.rem(self.chip + j % self.chips, self.chips) * 2 + (1 - self.core)
            self.arrived(x, y)
            return beside(x, y, running)

        return lax.fori_loop(0, self.nx * self.chips, one, carry)

    def finish(self):
        for copy in self.sent:
            copy.wait_send()


def fused_kernel(
    nx, ny, spans, total, block_ref, cols_ref, rows_ref, short_ref, geo_ref, codes_ref,
    counts_ref, gd_ref, gp_ref, rw_ref, emb_ref, cw_ref, owner_ref,
    energy_ref, force_ref,
    charge_ref, struct_ref, waves_ref, slices_ref, pair_ref, onehot_ref, gd_rows_ref,
    acc_ref, ghost_ref, back_ref,
    line1, cross1, pair1, recv1, line2, cross2, pair2, recv2, swap_send, swap_recv,
):
    slots, atoms = codes_ref.shape
    species, channels = emb_ref.shape
    basis = rw_ref.shape[0]
    wave_blocks = rows_ref.shape[0]
    gx, gy = lax.axis_index("gx"), lax.axis_index("gy")
    mine = gx * ny + gy

    def other(sx, sy):
        return {"gx": lax.rem(gx + sx + nx, nx), "gy": lax.rem(gy + sy + ny, ny)}

    barrier = pltpu.get_barrier_semaphore()
    steps = {(sx, 0) for sx in range(1, nx)} | {(0, sy) for sy in range(1, ny)}
    steps |= {(sx % nx, sy % ny) for sx, sy in DIRECTIONS}
    for sx, sy in sorted(steps):
        pl.semaphore_signal(barrier, inc=1, device_id=other(sx, sy), device_id_type=MESH)
    charge_ref[gx, gy] = block_ref[...]
    pl.semaphore_wait(barrier, len(steps))
    first = Spread(nx, ny, charge_ref, line1, cross1, pair1, recv1)
    second = Spread(nx, ny, struct_ref, line2, cross2, pair2, recv2)
    first.start()

    def table(cols, placed):
        turns = cols[:, 0:1] * (placed[0:1] * (1.0 / spans[0]))
        turns = turns + cols[:, 1:2] * (placed[1:2] * (1.0 / spans[1]))
        turns = turns + cols[:, 2:3] * (placed[2:3] * (1.0 / spans[2]))
        cosine, sine = cos_sin_turns(turns)
        return split_bf16(jnp.concatenate([cosine, sine], axis=0))

    own_placed = block_ref[channels:, :]

    def own_waves(w, carry):
        cols = cols_ref[pl.ds(pl.multiple_of(w * LANES, LANES), LANES), :]
        high, low = table(cols, own_placed)
        waves_ref[w, 0] = high
        waves_ref[w, 1] = low
        return carry

    def slice_waves(x, y):
        cols = cols_ref[pl.ds(pl.multiple_of(mine * LANES, LANES), LANES), :]
        high, low = table(cols, charge_ref[x, y, channels:, :])
        slices_ref[x, y, 0] = high
        slices_ref[x, y, 1] = low

    slice_waves(gx, gy)
    early = wave_blocks * 3 // 8
    lax.fori_loop(0, early, own_waves, 0)
    first.take_lines(lambda row, x, y: slice_waves(x, y))
    first.take_crosses(lambda row, x, y: slice_waves(x, y))

    def take_charge(x, y, carry):
        slice_waves(x, y)
        return carry

    first.take_pairs(take_charge, 0)

    summed = lax.fori_loop(
        0,
        wave_blocks,
        lambda d, running: running + charge_ref[d // ny, d % ny, :channels, :],
        jnp.zeros((channels, atoms), F32),
    )
    mean = jnp.sum(summed, axis=1, keepdims=True) / total

    def split_dot(a_high, a_low, b_high, b_low, dims):
        dot = functools.partial(
            lax.dot_general, dimension_numbers=(dims, ((), ())), preferred_element_type=F32
        )
        return dot(a_high, b_high) + (dot(a_high, b_low) + dot(a_low, b_high))

    def add_domain(d, running):
        x, y = d // ny, d % ny
        high, low = split_bf16(charge_ref[x, y, :channels, :] - mean)
        return running + split_dot(
            high, low, slices_ref[x, y, 0], slices_ref[x, y, 1], ((1,), (1,))
        )

    factors = lax.fori_loop(
        0, wave_blocks, add_domain, jnp.zeros((channels, 2 * LANES), F32), unroll=2
    )
    rows = rows_ref[mine]
    squared = jnp.zeros((1, LANES), F32)
    for x in range(3):
        wave = rows[x : x + 1] * (2.0 * math.pi / spans[x])
        squared = squared + wave * wave
    weight = jnp.exp(-0.5 * SCREENING * SCREENING * squared) / (squared + 1.0)
    weight = weight * (1.0 / math.sqrt(total))
    struct_ref[gx, gy] = factors * jnp.concatenate([weight, weight], axis=1)
    second.start()

    def near_rows(i):
        start = pl.multiple_of(i * SUBLANES, SUBLANES)
        window = pl.ds(start, SUBLANES)
        unit = [geo_ref[x, window, :] for x in range(3)]
        radius = geo_ref[3, window, :]
        kind = geo_ref[4, window, :]
        masks = [kind == float(s) for s in range(1, species)]
        slot = lax.broadcasted_iota(jnp.int32, (SUBLANES, atoms), 0) + start
        live = jnp.where(slot < counts_ref[...], 1.0, 0.0)

        def of_kind(rows):
            chosen = jnp.broadcast_to(rows[0:1, :], (SUBLANES, atoms))
            for s in range(1, species):
                chosen = jnp.where(masks[s - 1], rows[s : s + 1, :], chosen)
            return chosen

        def radial_of(b):
            offset = radius - BASIS_STEP * b
            radial = jnp.exp(-BASIS_WIDTH * (offset * offset)) * live
            return radial, (-2.0 * BASIS_WIDTH) * offset * radial

        return window, unit, radius, of_kind, radial_of

    gd_rows_ref[...] = gd_ref[...].reshape(basis, species, atoms)

    def short_pairs(i, carry):
        window, unit, radius, of_kind, radial_of = near_rows(i)
        along = jnp.zeros((SUBLANES, atoms), F32)
        turn = [jnp.zeros((SUBLANES, atoms), F32) for x in range(3)]
        for b in range(basis):
            radial, slope = radial_of(b)
            whole = of_kind(gd_rows_ref[b])
            for x in range(3):
                polar = of_kind(gp_ref[x * basis + b])
                whole = whole + unit[x] * polar
                turn[x] = turn[x] + radial * polar
            along = along + slope * whole
        inverse = 1.0 / radius
        swing = turn[0] * unit[0] + turn[1] * unit[1] + turn[2] * unit[2]
        radial_part = along - swing * inverse
        for x in range(3):
            pair_ref[x, window, :] = unit[x] * radial_part + turn[x] * inverse
        return carry

    def spots(n, carry):
        low = codes_ref[pl.ds(n, 1), :] % LANES
        ids = lax.broadcasted_iota(jnp.int32, (LANES, atoms), 0)
        onehot_ref[n] = jnp.where(ids == low, 1.0, 0.0).astype(BF16)
        return carry

    cuts = [early + (wave_blocks - early) * k // nx for k in range(nx + 1)]
    lax.fori_loop(cuts[0], cuts[1], own_waves, 0)
    second.take_lines(
        lambda row, x, y: lax.fori_loop(cuts[row + 1], cuts[row + 2], own_waves, 0)
    )
    groups = slots // SUBLANES
    shares = [groups * k // nx for k in range(nx + 1)]
    second.take_crosses(
        lambda row, x, y: lax.fori_loop(shares[row], shares[row + 1], short_pairs, 0)
    )
    lax.fori_loop(0, slots, spots, 0, unroll=2)

    neutral = block_ref[:channels, :] - mean
    neutral_high, neutral_low = split_bf16(neutral)

    def add_waves(x, y, carry):
        potential, pulled = carry
        w = x * ny + y
        high, low = waves_ref[w, 0], waves_ref[w, 1]
        s_high, s_low = split_bf16(struct_ref[x, y])
        potential = potential + split_dot(s_high, s_low, high, low, ((1,), (0,)))
        projected = split_dot(s_high, s_low, neutral_high, neutral_low, ((0,), (0,)))
        waves = high.astype(F32) + low.astype(F32)
        torque = waves[:LANES] * projected[LANES:] - waves[LANES:] * projected[:LANES]
        return potential, pulled + dot3(rows_ref[w], torque, ((1,), (0,)))

    chips = ny // 2
    core, chip = lax.rem(gy, 2), gy // 2

    def same_core(j, carry):
        return add_waves(
            lax.rem(gx + j // chips, nx), lax.rem(chip + j % chips, chips) * 2 + core, carry
        )

    carry = (jnp.zeros((channels, atoms), F32), jnp.zeros((SUBLANES, atoms), F32))
    carry = lax.fori_loop(0, nx * chips, same_core, carry)
    potential, pulled = second.take_pairs(add_waves, carry)

    energy_ref[...] = short_ref[...] + 0.5 * jnp.sum(neutral * potential, axis=0, keepdims=True)
    mixing = mixing_of(rw_ref[...], emb_ref[...])
    norm = 1.0 / math.sqrt(slots)
    density_grad = norm * dot_nn(mixing, dot_nn(cw_ref[...], potential))
    gd_rows_ref[...] = density_grad.reshape(basis, species, atoms)
    chunks = acc_ref.shape[0] // 6
    acc_ref[...] = jnp.zeros(acc_ref.shape, F32)
    chunk_ids = lax.broadcasted_iota(jnp.int32, (chunks, atoms), 0)

    def scatter_rows(i, centres):
        window, unit, radius, of_kind, radial_of = near_rows(i)
        along = jnp.zeros((SUBLANES, atoms), F32)
        for b in range(basis):
            along = along + radial_of(b)[1] * of_kind(gd_rows_ref[b])
        grads = [pair_ref[x, window, :] + unit[x] * along for x in range(3)]
        added = None
        high_codes = codes_ref[window, :] // LANES
        for k in range(SUBLANES):
            here = chunk_ids == high_codes[k : k + 1, :]
            values = jnp.concatenate(
                [jnp.where(here, grads[x][k : k + 1, :], 0.0) for x in range(3)], axis=0
            )
            part = lax.dot_general(
                jnp.concatenate(split_bf16(values), axis=0),
                onehot_ref[i * SUBLANES + k],
                (((1,), (1,)), ((), ())),
                preferred_element_type=F32,
            )
            added = part if added is None else added + part
        acc_ref[...] += added
        return tuple(centre + grad for centre, grad in zip(centres, grads))

    centres = lax.fori_loop(
        0, groups, scatter_rows, tuple(jnp.zeros((SUBLANES, atoms), F32) for x in range(3))
    )
    acc = acc_ref[: 3 * chunks, :] + acc_ref[3 * chunks :, :]
    own_chunks = atoms // LANES
    for d in range(len(DIRECTIONS)):
        picked = [acc[x * chunks + own_chunks + d : x * chunks + own_chunks + d + 1] for x in range(3)]
        filler = jnp.zeros((SUBLANES - 3, ghost_ref.shape[2]), F32)
        ghost_ref[d] = jnp.concatenate(picked + [filler], axis=0)
    swaps = [
        pltpu.make_async_remote_copy(
            src_ref=ghost_ref.at[d],
            dst_ref=back_ref.at[d],
            send_sem=swap_send.at[d],
            recv_sem=swap_recv.at[d],
            device_id=other(-sx, -sy),
            device_id_type=MESH,
        )
        for d, (sx, sy) in enumerate(DIRECTIONS)
    ]
    for swap in swaps:
        swap.start()
    rows = []
    for x in range(3):
        received = jnp.concatenate(
            [acc[x * chunks + h : x * chunks + h + 1, :] for h in range(own_chunks)], axis=1
        )
        centre = jnp.sum(centres[x], axis=0, keepdims=True)
        rows.append(received - centre + pulled[x : x + 1, :] * (2.0 * math.pi / spans[x]))
    sums = jnp.concatenate(rows + [jnp.zeros((SUBLANES - 3, atoms), F32)], axis=0)
    first.finish()
    second.finish()
    for d, swap in enumerate(swaps):
        swap.wait()
        sums = sums + owned(back_ref[d], owner_ref[d : d + 1, :], atoms)
    force_ref[...] = -sums[:3]


def spread_semaphores(nx, ny):
    chips = ny // 2
    return [
        pltpu.SemaphoreType.DMA((nx - 1,)),
        pltpu.SemaphoreType.DMA((nx, max(chips - 1, 1))),
        pltpu.SemaphoreType.DMA((nx, chips)),
        pltpu.SemaphoreType.DMA((nx, ny)),
    ]


def fused_call(nx, ny, spans, total, chunks, outs, *args):
    block, cols, rows, short, geo, codes, counts, gd, gp, rw, emb, cw, owner = args
    slots, atoms = codes.shape
    species, channels = emb.shape
    directions, width = owner.shape
    scratch = [
        pltpu.VMEM((nx, ny) + block.shape, F32),
        pltpu.VMEM((nx, ny, channels, 2 * LANES), F32),
        pltpu.VMEM((rows.shape[0], 2, 2 * LANES, atoms), BF16),
        pltpu.VMEM((nx, ny, 2, 2 * LANES, atoms), BF16),
        pltpu.VMEM((3, slots, atoms), F32),
        pltpu.VMEM((slots, LANES, atoms), BF16),
        pltpu.VMEM((rw.shape[0], species, atoms), F32),
        pltpu.VMEM((6 * chunks, LANES), F32),
        pltpu.VMEM((directions, SUBLANES, width), F32),
        pltpu.VMEM((directions, SUBLANES, width), F32),
    ]
    scratch += spread_semaphores(nx, ny) + spread_semaphores(nx, ny)
    scratch += [pltpu.SemaphoreType.DMA((directions,)), pltpu.SemaphoreType.DMA((directions,))]
    return pl.pallas_call(
        functools.partial(fused_kernel, nx, ny, spans, total),
        name="charges_to_forces",
        out_shape=[jax.ShapeDtypeStruct(shape, F32) for shape in outs],
        in_specs=[pl.BlockSpec(memory_space=VMEM)] * len(args),
        out_specs=[pl.BlockSpec(memory_space=VMEM)] * len(outs),
        scratch_shapes=scratch,
        compiler_params=pltpu.CompilerParams(
            collective_id=1, has_side_effects=True, vmem_limit_bytes=VMEM_LIMIT
        ),
    )(*args)


def local_call(kernel, name, outs, scratch, *args):
    return pl.pallas_call(
        kernel,
        name=name,
        out_shape=[jax.ShapeDtypeStruct(shape, F32) for shape in outs],
        in_specs=[pl.BlockSpec(memory_space=VMEM)] * len(args),
        out_specs=[pl.BlockSpec(memory_space=VMEM)] * len(outs),
        scratch_shapes=[pltpu.VMEM(shape, F32) for shape in scratch],
        compiler_params=pltpu.CompilerParams(vmem_limit_bytes=VMEM_LIMIT),
    )(*args)


def on_device(
    positions,
    species,
    neighbours,
    counts,
    ghost_list,
    wave_index,
    embedding,
    radial_weight,
    product_weight,
    readout_weight,
    charge_weight,
):
    nx, ny = lax.axis_size("gx"), lax.axis_size("gy")
    domains = nx * ny
    atoms = positions.shape[3]
    codes = neighbours[0, 0]
    slots = codes.shape[0]
    used = counts[0]
    ghost_rows = ghost_list[0, 0]
    directions, width = ghost_rows.shape
    waves = wave_index.shape[1]
    kinds, channels = embedding.shape
    basis = radial_weight.shape[0]
    spans = (float(nx), float(ny), SLAB_HEIGHT)
    total_atoms = float(atoms * domains)
    gx, gy = lax.axis_index("gx"), lax.axis_index("gy")
    record = jnp.concatenate(
        [positions.reshape(3, atoms), species[0].astype(F32)], axis=0
    )
    anchor = jnp.stack([gx.astype(F32), gy.astype(F32), jnp.zeros((), F32)]).reshape(3, 1)
    wave_float = wave_index.astype(F32)
    wave_cols = wave_float.T
    wave_rows = jnp.pad(
        wave_float.reshape(3, waves // LANES, LANES).transpose(1, 0, 2), ((0, 0), (0, 5), (0, 0))
    )
    readout = readout_weight.reshape(channels, 1)

    (outgoing,) = local_call(
        pick_kernel, "pick_ghosts", [(directions, SUBLANES, width)], [], record, ghost_rows
    )
    ghosts = swap_blocks(outgoing, 1, nx, ny, 0)
    block, short_energy, geometry, density_grad, polar_grad = local_call(
        short_kernel,
        "short_range",
        [
            (channels + SUBLANES, atoms),
            (1, atoms),
            (5, slots, atoms),
            (basis * kinds, atoms),
            (3 * basis, kinds, atoms),
        ],
        [(4 * basis, slots, atoms), (4 * basis, kinds, atoms)],
        record, ghosts, codes, used, anchor,
        embedding, radial_weight, product_weight, readout, charge_weight,
    )
    wave_blocks = waves // LANES
    chunks = 16 * -(-(atoms // LANES + directions * width // LANES) // 16)
    if wave_blocks == domains:
        energy, forces = fused_call(
            nx, ny, spans, total_atoms, chunks, [(1, atoms), (3, atoms)],
            block, wave_cols, wave_rows, short_energy, geometry, codes, used,
            density_grad, polar_grad, radial_weight, embedding, charge_weight, ghost_rows,
        )
        return (forces[:, None, None, :], energy[None])
    charge_total = lax.psum(jnp.sum(block[:channels], axis=1, keepdims=True), ("gx", "gy"))
    mean = jnp.broadcast_to(charge_total / total_atoms, (channels, LANES))
    neutral = jnp.concatenate([block[:channels] - mean[:, :1], block[channels:]], axis=0)
    (struct,) = local_call(
        functools.partial(structure_kernel, total_atoms, channels, spans),
        "structure",
        [(wave_blocks, channels, 2 * LANES)],
        [],
        neutral,
        wave_cols,
        wave_rows,
    )
    struct = lax.psum(struct, ("gx", "gy"))
    energy, own_grad, ghost_grad = local_call(
        functools.partial(back_kernel, spans),
        "gradients",
        [(1, atoms), (SUBLANES, atoms), (directions, SUBLANES, width)],
        [(basis, kinds, atoms), (3, slots, atoms), (6 * chunks, LANES)],
        struct, wave_cols, wave_rows, block, mean, short_energy, geometry, codes, used,
        density_grad, polar_grad, radial_weight, embedding, charge_weight,
    )
    back = swap_blocks(ghost_grad, -1, nx, ny, 3)
    (forces,) = local_call(owners_kernel, "owners", [(3, atoms)], [], back, ghost_rows, own_grad)
    return (forces[:, None, None, :], energy[None])


def solution(mesh):
    in_specs = (
        P(None, ("group", "gx"), "gy", None),
        P(("group", "gx"), "gy", None),
        P(("group", "gx"), "gy", None, None),
        P(("group", "gx"), "gy", None),
        P(("group", "gx"), "gy", None, None),
        P(),
        P(),
        P(),
        P(),
        P(),
        P(),
    )
    out_specs = (P(None, ("group", "gx"), "gy", None), P(("group", "gx"), "gy", None))
    return jax.shard_map(
        on_device, mesh=mesh, in_specs=in_specs, out_specs=out_specs, check_vma=False
    )
```

```python
import functools
import math

import jax
import jax.numpy as jnp
import numpy as np
from jax import lax
from jax.experimental import pallas as pl
from jax.experimental.pallas import tpu as pltpu
from jax.sharding import PartitionSpec as P

DIRECTIONS = ((-1, -1), (-1, 0), (-1, 1), (0, -1), (0, 1), (1, -1), (1, 0), (1, 1))
SOFTENING = 0.01
BASIS_WIDTH = 2.0
BASIS_STEP = 0.35
SCREENING = 0.02
SLAB_HEIGHT = 2.0
PRECISE = lax.Precision.HIGHEST
MESH = pl.DeviceIdType.MESH
LANES = 128
SUBLANES = 8
VMEM_LIMIT = 40 * 1024 * 1024
F32 = jnp.float32
BF16 = jnp.bfloat16
VMEM = pltpu.VMEM


def half_turn_series(odd, terms):
    nodes = 0.125 * (1.0 + np.cos(np.pi * (np.arange(64) + 0.5) / 64))
    root = np.sqrt(nodes)
    values = np.sin(np.pi * root) / root if odd else np.cos(np.pi * root)
    series = np.polynomial.chebyshev.Chebyshev.fit(nodes, values, terms - 1, domain=[0.0, 0.25])
    return [float(c) for c in series.convert(kind=np.polynomial.Polynomial).coef]


SIN_SERIES = half_turn_series(True, 6)
COS_SERIES = half_turn_series(False, 6)


def horner(series, square):
    total = jnp.full_like(square, series[-1])
    for coefficient in reversed(series[:-1]):
        total = total * square + coefficient
    return total


def cos_sin_turns(turns):
    reduced = turns - jnp.round(turns)
    square = reduced * reduced
    half_sin = reduced * horner(SIN_SERIES, square)
    half_cos = horner(COS_SERIES, square)
    return 1.0 - 2.0 * (half_sin * half_sin), 2.0 * (half_sin * half_cos)


def dot_nn(a, b):
    return lax.dot_general(
        a, b, (((1,), (0,)), ((), ())), precision=PRECISE, preferred_element_type=F32
    )


def dot_tn(a, b):
    return lax.dot_general(
        a, b, (((0,), (0,)), ((), ())), precision=PRECISE, preferred_element_type=F32
    )


def split_bf16(value):
    high = value.astype(BF16)
    return high, (value - high.astype(F32)).astype(BF16)


def dot3(a, b, dims):
    a_high, a_low = split_bf16(a)
    b_high, b_low = split_bf16(b)
    dot = functools.partial(
        lax.dot_general, dimension_numbers=(dims, ((), ())), preferred_element_type=F32
    )
    return dot(a_high, b_high) + (dot(a_high, b_low) + dot(a_low, b_high))


def lookup(table_row, codes):
    rows = codes.shape[0]
    pieces = []
    for part in range(codes.shape[1] // LANES):
        code = codes[:, part * LANES : (part + 1) * LANES]
        low, high = code % LANES, code // LANES
        found = jnp.zeros((rows, LANES), F32)
        for chunk in range(table_row.shape[1] // LANES):
            table = jnp.broadcast_to(
                table_row[:, chunk * LANES : (chunk + 1) * LANES], (rows, LANES)
            )
            picked = jnp.take_along_axis(table, low, axis=1)
            found = jnp.where(high == chunk, picked, found)
        pieces.append(found)
    return jnp.concatenate(pieces, axis=1)


def pick_kernel(record_ref, rows_ref, out_ref):
    rows = rows_ref[...]
    for field in range(4):
        found = lookup(record_ref[field : field + 1, :], rows)
        for direction, shift in enumerate(DIRECTIONS):
            offset = float(shift[field]) if field < 2 else 0.0
            out_ref[direction, field : field + 1, :] = found[direction : direction + 1] - offset
    for direction in range(len(DIRECTIONS)):
        out_ref[direction, 4:, :] = jnp.zeros((4, rows.shape[1]), F32)


def swap_kernel(sign, nx, ny, in_ref, out_ref, send_sem, recv_sem):
    gx, gy = lax.axis_index("gx"), lax.axis_index("gy")
    targets = [
        {
            "gx": lax.rem(gx + sign * sx + nx, nx),
            "gy": lax.rem(gy + sign * sy + ny, ny),
        }
        for sx, sy in DIRECTIONS
    ]
    barrier = pltpu.get_barrier_semaphore()
    for target in targets:
        pl.semaphore_signal(barrier, inc=1, device_id=target, device_id_type=MESH)
    pl.semaphore_wait(barrier, len(targets))
    copies = [
        pltpu.make_async_remote_copy(
            src_ref=in_ref.at[d],
            dst_ref=out_ref.at[d],
            send_sem=send_sem.at[d],
            recv_sem=recv_sem.at[d],
            device_id=target,
            device_id_type=MESH,
        )
        for d, target in enumerate(targets)
    ]
    for copy in copies:
        copy.start()
    for copy in copies:
        copy.wait()


def swap_blocks(blocks, sign, nx, ny, collective_id):
    count = blocks.shape[0]
    return pl.pallas_call(
        functools.partial(swap_kernel, sign, nx, ny),
        name="ghosts_out" if sign == 1 else "ghosts_back",
        out_shape=jax.ShapeDtypeStruct(blocks.shape, F32),
        in_specs=[pl.BlockSpec(memory_space=VMEM)],
        out_specs=pl.BlockSpec(memory_space=VMEM),
        scratch_shapes=[pltpu.SemaphoreType.DMA((count,)), pltpu.SemaphoreType.DMA((count,))],
        compiler_params=pltpu.CompilerParams(collective_id=collective_id, has_side_effects=True),
    )(blocks)


def mixing_of(radial_weight, embedding):
    return jnp.concatenate(
        [radial_weight[b : b + 1, :] * embedding for b in range(radial_weight.shape[0])], axis=0
    )


def short_kernel(
    record_ref, ghost_ref, codes_ref, counts_ref, anchor_ref,
    emb_ref, rw_ref, pw_ref, ro_ref, cw_ref,
    block_ref, energy_ref, geo_ref, gd_ref, gp_ref,
    terms_ref, moments_ref,
):
    slots, atoms = codes_ref.shape
    species, channels = emb_ref.shape
    basis = rw_ref.shape[0]
    codes = codes_ref[...]
    near = []
    for field in range(4):
        row = jnp.concatenate(
            [record_ref[field : field + 1, :]]
            + [ghost_ref[d, field : field + 1, :] for d in range(ghost_ref.shape[0])],
            axis=1,
        )
        near.append(lookup(row, codes))
    separation = [near[x] - record_ref[x : x + 1, :] for x in range(3)]
    square = separation[0] * separation[0]
    square = square + separation[1] * separation[1] + separation[2] * separation[2]
    radius = jnp.sqrt(square + SOFTENING)
    inverse = 1.0 / radius
    kind = near[3]
    slot = lax.broadcasted_iota(jnp.int32, (slots, atoms), 0)
    live = jnp.where(slot < counts_ref[...], 1.0, 0.0)
    unit = [part * inverse for part in separation]
    for x in range(3):
        geo_ref[x] = unit[x]
    geo_ref[3] = radius
    geo_ref[4] = kind
    for b in range(basis):
        offset = radius - BASIS_STEP * b
        radial = jnp.exp(-BASIS_WIDTH * (offset * offset)) * live
        terms_ref[b] = radial
        for x in range(3):
            terms_ref[(x + 1) * basis + b] = unit[x] * radial

    def reduce_term(q, carry):
        term = terms_ref[q]
        near_kind = geo_ref[4]
        rows = [
            jnp.sum(jnp.where(near_kind == float(s), term, 0.0), axis=0, keepdims=True)
            for s in range(species)
        ]
        moments_ref[q] = jnp.concatenate(rows, axis=0)
        return carry

    lax.fori_loop(0, 4 * basis, reduce_term, 0, unroll=2)
    mixing = mixing_of(rw_ref[...], emb_ref[...])
    norm = 1.0 / math.sqrt(slots)
    moments = [
        moments_ref[q * basis : (q + 1) * basis].reshape(basis * species, atoms) for q in range(4)
    ]
    own_species = lax.broadcasted_iota(jnp.int32, (species, atoms), 0).astype(F32)
    onehot = jnp.where(own_species == record_ref[3:4, :], 1.0, 0.0)
    scalar = norm * dot_tn(mixing, moments[0]) + dot_tn(emb_ref[...], onehot)
    vectorial = [norm * dot_tn(mixing, moments[x + 1]) for x in range(3)]
    squares = vectorial[0] * vectorial[0] + vectorial[1] * vectorial[1] + vectorial[2] * vectorial[2]
    invariants = jnp.concatenate([scalar, squares], axis=0)
    before = dot_tn(pw_ref[...], invariants)
    gate = 1.0 / (1.0 + jnp.exp(-before))
    hidden = before * gate
    energy_ref[...] = jnp.sum(hidden * ro_ref[...], axis=0, keepdims=True)
    block_ref[:channels, :] = dot_tn(cw_ref[...], scalar)
    block_ref[channels : channels + 3, :] = record_ref[:3, :] + anchor_ref[...]
    block_ref[channels + 3 :, :] = jnp.zeros((SUBLANES - 3, atoms), F32)
    slope = ro_ref[...] * (gate + hidden * (1.0 - gate))
    back = dot_nn(pw_ref[...], slope)
    gd_ref[...] = norm * dot_nn(mixing, back[:channels])
    for x in range(3):
        grad = norm * dot_nn(mixing, 2.0 * vectorial[x] * back[channels:])
        gp_ref[x * basis : (x + 1) * basis] = grad.reshape(basis, species, atoms)


def structure_kernel(total, channels, spans, block_ref, cols_ref, rows_ref, out_ref):
    def one_block(w, carry):
        cols = cols_ref[pl.ds(pl.multiple_of(w * LANES, LANES), LANES), :]
        turns = jnp.zeros((LANES, block_ref.shape[1]), F32)
        for x in range(3):
            placed = block_ref[channels + x : channels + x + 1, :]
            turns = turns + cols[:, x : x + 1] * (placed * (1.0 / spans[x]))
        waves = jnp.concatenate(cos_sin_turns(turns), axis=0)
        rows = rows_ref[w]
        squared = jnp.zeros((1, LANES), F32)
        for x in range(3):
            wave = rows[x : x + 1] * (2.0 * math.pi / spans[x])
            squared = squared + wave * wave
        weight = jnp.exp(-0.5 * SCREENING * SCREENING * squared) / (squared + 1.0)
        weight = weight * (1.0 / math.sqrt(total))
        factors = dot3(block_ref[:channels, :], waves, ((1,), (1,)))
        out_ref[w] = factors * jnp.concatenate([weight, weight], axis=1)
        return carry

    lax.fori_loop(0, out_ref.shape[0], one_block, 0)


def back_kernel(
    spans, struct_ref, cols_ref, rows_ref, block_ref, mean_ref, short_ref, geo_ref, codes_ref,
    counts_ref, gd_ref, gp_ref, rw_ref, emb_ref, cw_ref,
    energy_ref, own_ref, ghost_ref,
    gd_rows_ref, pair_ref, acc_ref,
):
    slots, atoms = codes_ref.shape
    species, channels = emb_ref.shape
    basis = rw_ref.shape[0]
    wave_blocks = struct_ref.shape[0]
    neutral = block_ref[:channels, :] - mean_ref[:, 0:1]
    neutral_high, neutral_low = split_bf16(neutral)
    scaled = [block_ref[channels + x : channels + x + 1, :] * (1.0 / spans[x]) for x in range(3)]
    over_rows = ((0,), (0,))

    def add_waves(w, carry):
        potential, pulled = carry
        cols = cols_ref[pl.ds(pl.multiple_of(w * LANES, LANES), LANES), :]
        turns = cols[:, 0:1] * scaled[0] + cols[:, 1:2] * scaled[1] + cols[:, 2:3] * scaled[2]
        cosine, sine = cos_sin_turns(turns)
        waves = jnp.concatenate([cosine, sine], axis=0)
        struct = struct_ref[w]
        potential = potential + dot3(struct, waves, ((1,), (0,)))
        high, low = split_bf16(struct)
        dot = functools.partial(
            lax.dot_general, dimension_numbers=(over_rows, ((), ())), preferred_element_type=F32
        )
        projected = dot(high, neutral_high) + (dot(high, neutral_low) + dot(low, neutral_high))
        torque = cosine * projected[LANES:] - sine * projected[:LANES]
        return potential, pulled + dot3(rows_ref[w], torque, ((1,), (0,)))

    potential, pulled = lax.fori_loop(
        0,
        wave_blocks,
        add_waves,
        (jnp.zeros((channels, atoms), F32), jnp.zeros((SUBLANES, atoms), F32)),
    )
    energy_ref[...] = short_ref[...] + 0.5 * jnp.sum(neutral * potential, axis=0, keepdims=True)
    mixing = mixing_of(rw_ref[...], emb_ref[...])
    norm = 1.0 / math.sqrt(slots)
    density_grad = gd_ref[...] + norm * dot_nn(mixing, dot_nn(cw_ref[...], potential))
    gd_rows_ref[...] = density_grad.reshape(basis, species, atoms)

    def pair_rows(i, carry):
        start = pl.multiple_of(i * SUBLANES, SUBLANES)
        window = pl.ds(start, SUBLANES)
        unit = [geo_ref[x, window, :] for x in range(3)]
        radius = geo_ref[3, window, :]
        kind = geo_ref[4, window, :]
        masks = [kind == float(s) for s in range(1, species)]
        slot = lax.broadcasted_iota(jnp.int32, (SUBLANES, atoms), 0) + start
        live = jnp.where(slot < counts_ref[...], 1.0, 0.0)

        def of_kind(table):
            chosen = jnp.broadcast_to(table[0:1, :], (SUBLANES, atoms))
            for s in range(1, species):
                chosen = jnp.where(masks[s - 1], table[s : s + 1, :], chosen)
            return chosen

        along = jnp.zeros((SUBLANES, atoms), F32)
        turn = [jnp.zeros((SUBLANES, atoms), F32) for x in range(3)]
        for b in range(basis):
            offset = radius - BASIS_STEP * b
            radial = jnp.exp(-BASIS_WIDTH * (offset * offset)) * live
            total = of_kind(gd_rows_ref[b])
            for x in range(3):
                polar = of_kind(gp_ref[x * basis + b])
                total = total + unit[x] * polar
                turn[x] = turn[x] + radial * polar
            along = along + (-2.0 * BASIS_WIDTH) * offset * radial * total
        inverse = 1.0 / radius
        swing = turn[0] * unit[0] + turn[1] * unit[1] + turn[2] * unit[2]
        radial_part = along - swing * inverse
        for x in range(3):
            pair_ref[x, window, :] = unit[x] * radial_part + turn[x] * inverse
        return carry

    lax.fori_loop(0, slots // SUBLANES, pair_rows, 0)
    chunks = acc_ref.shape[0] // 6
    acc_ref[...] = jnp.zeros(acc_ref.shape, F32)
    group = 4

    def scatter_rows(i, carry):
        start = i * group
        total = None
        for k in range(group):
            code = codes_ref[pl.ds(start + k, 1), :]
            low, high = code % LANES, code // LANES
            spots = lax.broadcasted_iota(jnp.int32, (LANES, atoms), 0)
            onehot = jnp.where(spots == low, 1.0, 0.0).astype(BF16)
            chunk_ids = lax.broadcasted_iota(jnp.int32, (chunks, atoms), 0)
            here = chunk_ids == high
            values = jnp.concatenate(
                [jnp.where(here, pair_ref[x, pl.ds(start + k, 1), :], 0.0) for x in range(3)],
                axis=0,
            )
            values = jnp.concatenate(split_bf16(values), axis=0)
            part = lax.dot_general(
                values, onehot, (((1,), (1,)), ((), ())), preferred_element_type=F32
            )
            total = part if total is None else total + part
        acc_ref[...] += total
        return carry

    lax.fori_loop(0, slots // group, scatter_rows, 0)
    summed = acc_ref[: 3 * chunks, :] + acc_ref[3 * chunks :, :]
    own_chunks = atoms // LANES
    own_ref[...] = jnp.zeros(own_ref.shape, F32)
    ghost_ref[...] = jnp.zeros(ghost_ref.shape, F32)
    for x in range(3):
        received = jnp.concatenate(
            [summed[x * chunks + h : x * chunks + h + 1, :] for h in range(own_chunks)], axis=1
        )
        centre = jnp.sum(pair_ref[x], axis=0, keepdims=True)
        wave_pull = pulled[x : x + 1, :] * (2.0 * math.pi / spans[x])
        own_ref[x : x + 1, :] = received - centre + wave_pull
        for d in range(ghost_ref.shape[0]):
            row = x * chunks + own_chunks + d
            ghost_ref[d, x : x + 1, :] = summed[row : row + 1, :]


def owned(values, rows, atoms):
    ids = lax.broadcasted_iota(jnp.int32, (atoms, rows.shape[1]), 0)
    onehot = jnp.where(ids == rows, 1.0, 0.0).astype(BF16)
    halves = jnp.concatenate(split_bf16(values), axis=0)
    part = lax.dot_general(halves, onehot, (((1,), (1,)), ((), ())), preferred_element_type=F32)
    return part[:SUBLANES] + part[SUBLANES:]


def owners_kernel(back_ref, rows_ref, own_ref, out_ref):
    total = own_ref[...]
    for d in range(back_ref.shape[0]):
        total = total + owned(back_ref[d], rows_ref[d : d + 1, :], own_ref.shape[1])
    out_ref[...] = -total[:3]


class Spread:
    def __init__(self, nx, ny, buffer, line_sem, cross_sem, pair_sem, recv_sem):
        self.gx, self.gy = lax.axis_index("gx"), lax.axis_index("gy")
        self.nx, self.chips = nx, ny // 2
        self.core = lax.rem(self.gy, 2)
        self.chip = self.gy // 2
        self.peer = self.chip * 2 + (1 - self.core)
        order = sorted(range(1, nx), key=lambda step: min(step, nx - step))
        self.lines = [lax.rem(self.gx + step, nx) for step in order]
        self.crosses = [
            lax.rem(self.chip + step, self.chips) * 2 + self.core for step in range(1, self.chips)
        ]
        self.buffer = buffer
        self.line_sem, self.cross_sem, self.pair_sem = line_sem, cross_sem, pair_sem
        self.recv_sem = recv_sem
        self.sent = []

    def remote(self, x, y, send_sem, device):
        return pltpu.make_async_remote_copy(
            src_ref=self.buffer.at[x, y],
            dst_ref=self.buffer.at[x, y],
            send_sem=send_sem,
            recv_sem=self.recv_sem.at[x, y],
            device_id=device,
            device_id_type=MESH,
        )

    def send(self, x, y, send_sem, device):
        copy = self.remote(x, y, send_sem, device)
        copy.start()
        self.sent.append(copy)

    def arrived(self, x, y):
        self.remote(x, y, self.line_sem.at[0], {"gy": self.peer}).wait_recv()

    def to_chip(self, x, row):
        for index, y in enumerate(self.crosses):
            self.send(x, self.gy, self.cross_sem.at[row, index], {"gy": y})
        self.send(x, self.gy, self.pair_sem.at[row, 0], {"gy": self.peer})

    def start(self):
        for index, x in enumerate(self.lines):
            self.send(self.gx, self.gy, self.line_sem.at[index], {"gx": x})
        self.to_chip(self.gx, 0)

    def take_lines(self, beside):
        for row, x in enumerate(self.lines):
            self.arrived(x, self.gy)
            self.to_chip(x, row + 1)
            beside(row, x, self.gy)

    def take_crosses(self, beside):
        for row, x in enumerate([self.gx] + self.lines):
            for index, y in enumerate(self.crosses):
                self.arrived(x, y)
                self.send(x, y, self.pair_sem.at[row, index + 1], {"gy": self.peer})
                beside(row, x, y)

    def take_pairs(self, beside, carry):
        def one(j, running):
            x = lax.rem(self.gx + j // self.chips, self.nx)
            y = lax.rem(self.chip + j % self.chips, self.chips) * 2 + (1 - self.core)
            self.arrived(x, y)
            return beside(x, y, running)

        return lax.fori_loop(0, self.nx * self.chips, one, carry)

    def finish(self):
        for copy in self.sent:
            copy.wait_send()


def fused_kernel(
    nx, ny, spans, total, block_ref, cols_ref, rows_ref, short_ref, geo_ref, codes_ref,
    counts_ref, gd_ref, gp_ref, rw_ref, emb_ref, cw_ref, owner_ref,
    energy_ref, force_ref,
    charge_ref, struct_ref, waves_ref, wide_ref, slim_ref, sum_ref, long_ref, pair_ref, onehot_ref, gd_rows_ref,
    acc_ref, ghost_ref, back_ref,
    line1, cross1, pair1, recv1, line2, cross2, pair2, recv2, swap_send, swap_recv,
):
    slots, atoms = codes_ref.shape
    species, channels = emb_ref.shape
    basis = rw_ref.shape[0]
    wave_blocks = rows_ref.shape[0]
    gx, gy = lax.axis_index("gx"), lax.axis_index("gy")
    mine = gx * ny + gy

    def other(sx, sy):
        return {"gx": lax.rem(gx + sx + nx, nx), "gy": lax.rem(gy + sy + ny, ny)}

    barrier = pltpu.get_barrier_semaphore()
    steps = {(sx, 0) for sx in range(1, nx)} | {(0, sy) for sy in range(1, ny)}
    steps |= {(sx % nx, sy % ny) for sx, sy in DIRECTIONS}
    for sx, sy in sorted(steps):
        pl.semaphore_signal(barrier, inc=1, device_id=other(sx, sy), device_id_type=MESH)
    charge_ref[gx, gy] = block_ref[...]
    pl.semaphore_wait(barrier, len(steps))
    first = Spread(nx, ny, charge_ref, line1, cross1, pair1, recv1)
    second = Spread(nx, ny, struct_ref, line2, cross2, pair2, recv2)
    first.start()

    def table(cols, placed):
        turns = cols[:, 0:1] * (placed[0:1] * (1.0 / spans[0]))
        turns = turns + cols[:, 1:2] * (placed[1:2] * (1.0 / spans[1]))
        turns = turns + cols[:, 2:3] * (placed[2:3] * (1.0 / spans[2]))
        cosine, sine = cos_sin_turns(turns)
        return split_bf16(jnp.concatenate([cosine, sine], axis=0))

    own_placed = block_ref[channels:, :]

    def own_waves(w, carry):
        cols = cols_ref[pl.ds(pl.multiple_of(w * LANES, LANES), LANES), :]
        high, low = table(cols, own_placed)
        waves_ref[w, 0] = high
        waves_ref[w, 1] = low
        return carry

    shift = jnp.sum(block_ref[:channels, :], axis=1, keepdims=True) * (1.0 / atoms)
    ones = jnp.ones((channels, atoms), BF16)
    blank = jnp.zeros((channels, atoms), BF16)
    wide_ref[...] = jnp.zeros(wide_ref.shape, F32)
    slim_ref[...] = jnp.zeros(slim_ref.shape, F32)
    sum_ref[...] = jnp.zeros(sum_ref.shape, F32)

    def over_atoms(a, b):
        return lax.dot_general(a, b, (((1,), (1,)), ((), ())), preferred_element_type=F32)

    def slice_waves(x, y):
        cols = cols_ref[pl.ds(pl.multiple_of(mine * LANES, LANES), LANES), :]
        high, low = table(cols, charge_ref[x, y, channels:, :])
        charges = charge_ref[x, y, :channels, :]
        sum_ref[...] += charges
        q_high, q_low = split_bf16(charges - shift)
        wide_ref[...] += over_atoms(high, jnp.concatenate([q_high, ones, q_low, blank], axis=0))
        slim_ref[...] += over_atoms(low, jnp.concatenate([q_high, ones], axis=0))

    slice_waves(gx, gy)
    early = wave_blocks * 3 // 8
    lax.fori_loop(0, early, own_waves, 0)
    first.take_lines(lambda row, x, y: slice_waves(x, y))
    first.take_crosses(lambda row, x, y: slice_waves(x, y))

    def take_charge(x, y, carry):
        slice_waves(x, y)
        return carry

    first.take_pairs(take_charge, 0)

    mean = jnp.sum(sum_ref[...], axis=1, keepdims=True) / total
    wide = wide_ref[...]
    main = jnp.transpose(wide[:, : 2 * channels] + slim_ref[...])
    rest = jnp.transpose(wide[:, 2 * channels :])
    factors = main[:channels] + rest[:channels]
    factors = factors + (shift - mean) * main[channels : channels + 1]
    rows = rows_ref[mine]
    squared = jnp.zeros((1, LANES), F32)
    for x in range(3):
        wave = rows[x : x + 1] * (2.0 * math.pi / spans[x])
        squared = squared + wave * wave
    weight = jnp.exp(-0.5 * SCREENING * SCREENING * squared) / (squared + 1.0)
    weight = weight * (1.0 / math.sqrt(total))
    struct_ref[gx, gy] = factors * jnp.concatenate([weight, weight], axis=1)
    second.start()

    def near_rows(i):
        start = pl.multiple_of(i * SUBLANES, SUBLANES)
        window = pl.ds(start, SUBLANES)
        unit = [geo_ref[x, window, :] for x in range(3)]
        radius = geo_ref[3, window, :]
        kind = geo_ref[4, window, :]
        masks = [kind == float(s) for s in range(1, species)]
        slot = lax.broadcasted_iota(jnp.int32, (SUBLANES, atoms), 0) + start
        live = jnp.where(slot < counts_ref[...], 1.0, 0.0)

        def of_kind(rows):
            chosen = jnp.broadcast_to(rows[0:1, :], (SUBLANES, atoms))
            for s in range(1, species):
                chosen = jnp.where(masks[s - 1], rows[s : s + 1, :], chosen)
            return chosen

        def radial_of(b):
            offset = radius - BASIS_STEP * b
            radial = jnp.exp(-BASIS_WIDTH * (offset * offset)) * live
            return radial, (-2.0 * BASIS_WIDTH) * offset * radial

        return window, unit, radius, of_kind, radial_of

    gd_rows_ref[...] = gd_ref[...].reshape(basis, species, atoms)

    def short_pairs(i, carry):
        window, unit, radius, of_kind, radial_of = near_rows(i)
        along = jnp.zeros((SUBLANES, atoms), F32)
        turn = [jnp.zeros((SUBLANES, atoms), F32) for x in range(3)]
        for b in range(basis):
            radial, slope = radial_of(b)
            whole = of_kind(gd_rows_ref[b])
            for x in range(3):
                polar = of_kind(gp_ref[x * basis + b])
                whole = whole + unit[x] * polar
                turn[x] = turn[x] + radial * polar
            along = along + slope * whole
        inverse = 1.0 / radius
        swing = turn[0] * unit[0] + turn[1] * unit[1] + turn[2] * unit[2]
        radial_part = along - swing * inverse
        for x in range(3):
            pair_ref[x, window, :] = unit[x] * radial_part + turn[x] * inverse
        return carry

    def spots(n, carry):
        low = codes_ref[pl.ds(n, 1), :] % LANES
        ids = lax.broadcasted_iota(jnp.int32, (LANES, atoms), 0)
        onehot_ref[n] = jnp.where(ids == low, 1.0, 0.0).astype(BF16)
        return carry

    cuts = [early + (wave_blocks - early) * k // nx for k in range(nx + 1)]
    lax.fori_loop(cuts[0], cuts[1], own_waves, 0)
    second.take_lines(
        lambda row, x, y: lax.fori_loop(cuts[row + 1], cuts[row + 2], own_waves, 0)
    )
    groups = slots // SUBLANES
    shares = [groups * k // nx for k in range(nx + 1)]
    second.take_crosses(
        lambda row, x, y: lax.fori_loop(shares[row], shares[row + 1], short_pairs, 0)
    )
    lax.fori_loop(0, slots, spots, 0, unroll=2)

    neutral = block_ref[:channels, :] - mean
    long_ref[...] = jnp.zeros(long_ref.shape, F32)

    def add_waves(x, y, carry):
        w = x * ny + y
        struct = struct_ref[x, y]
        turned = jnp.concatenate([struct[:, LANES:], -struct[:, :LANES]], axis=1)
        rows = rows_ref[w]
        rows = jnp.concatenate([rows, rows], axis=1)
        parts = [struct] + [turned * rows[axis : axis + 1] for axis in range(3)]
        high, low = split_bf16(jnp.concatenate(parts, axis=0))
        both = jnp.dot(
            jnp.concatenate([high, low], axis=0), waves_ref[w, 0], preferred_element_type=F32
        )
        fine = jnp.dot(high, waves_ref[w, 1], preferred_element_type=F32)
        count = high.shape[0]
        long_ref[...] += both[:count] + both[count:] + fine
        return carry

    chips = ny // 2
    core, chip = lax.rem(gy, 2), gy // 2

    def same_core(j, carry):
        return add_waves(
            lax.rem(gx + j // chips, nx), lax.rem(chip + j % chips, chips) * 2 + core, carry
        )

    lax.fori_loop(0, nx * chips, same_core, 0)
    second.take_pairs(add_waves, 0)
    potential = long_ref[:channels, :]
    pulled = [
        jnp.sum(neutral * long_ref[(x + 1) * channels : (x + 2) * channels, :], axis=0, keepdims=True)
        for x in range(3)
    ]

    energy_ref[...] = short_ref[...] + 0.5 * jnp.sum(neutral * potential, axis=0, keepdims=True)
    mixing = mixing_of(rw_ref[...], emb_ref[...])
    norm = 1.0 / math.sqrt(slots)
    density_grad = norm * dot_nn(mixing, dot_nn(cw_ref[...], potential))
    gd_rows_ref[...] = density_grad.reshape(basis, species, atoms)
    chunks = acc_ref.shape[0] // 6
    acc_ref[...] = jnp.zeros(acc_ref.shape, F32)
    chunk_ids = lax.broadcasted_iota(jnp.int32, (chunks, atoms), 0)

    def scatter_rows(i, centres):
        window, unit, radius, of_kind, radial_of = near_rows(i)
        along = jnp.zeros((SUBLANES, atoms), F32)
        for b in range(basis):
            along = along + radial_of(b)[1] * of_kind(gd_rows_ref[b])
        grads = [pair_ref[x, window, :] + unit[x] * along for x in range(3)]
        added = None
        high_codes = codes_ref[window, :] // LANES
        for k in range(SUBLANES):
            here = chunk_ids == high_codes[k : k + 1, :]
            values = jnp.concatenate(
                [jnp.where(here, grads[x][k : k + 1, :], 0.0) for x in range(3)], axis=0
            )
            part = lax.dot_general(
                jnp.concatenate(split_bf16(values), axis=0),
                onehot_ref[i * SUBLANES + k],
                (((1,), (1,)), ((), ())),
                preferred_element_type=F32,
            )
            added = part if added is None else added + part
        acc_ref[...] += added
        return tuple(centre + grad for centre, grad in zip(centres, grads))

    centres = lax.fori_loop(
        0, groups, scatter_rows, tuple(jnp.zeros((SUBLANES, atoms), F32) for x in range(3))
    )
    acc = acc_ref[: 3 * chunks, :] + acc_ref[3 * chunks :, :]
    own_chunks = atoms // LANES
    for d in range(len(DIRECTIONS)):
        picked = [acc[x * chunks + own_chunks + d : x * chunks + own_chunks + d + 1] for x in range(3)]
        filler = jnp.zeros((SUBLANES - 3, ghost_ref.shape[2]), F32)
        ghost_ref[d] = jnp.concatenate(picked + [filler], axis=0)
    swaps = [
        pltpu.make_async_remote_copy(
            src_ref=ghost_ref.at[d],
            dst_ref=back_ref.at[d],
            send_sem=swap_send.at[d],
            recv_sem=swap_recv.at[d],
            device_id=other(-sx, -sy),
            device_id_type=MESH,
        )
        for d, (sx, sy) in enumerate(DIRECTIONS)
    ]
    for swap in swaps:
        swap.start()
    rows = []
    for x in range(3):
        received = jnp.concatenate(
            [acc[x * chunks + h : x * chunks + h + 1, :] for h in range(own_chunks)], axis=1
        )
        centre = jnp.sum(centres[x], axis=0, keepdims=True)
        rows.append(received - centre + pulled[x] * (2.0 * math.pi / spans[x]))
    sums = jnp.concatenate(rows + [jnp.zeros((SUBLANES - 3, atoms), F32)], axis=0)
    first.finish()
    second.finish()
    for d, swap in enumerate(swaps):
        swap.wait()
        sums = sums + owned(back_ref[d], owner_ref[d : d + 1, :], atoms)
    force_ref[...] = -sums[:3]


def spread_semaphores(nx, ny):
    chips = ny // 2
    return [
        pltpu.SemaphoreType.DMA((nx - 1,)),
        pltpu.SemaphoreType.DMA((nx, max(chips - 1, 1))),
        pltpu.SemaphoreType.DMA((nx, chips)),
        pltpu.SemaphoreType.DMA((nx, ny)),
    ]


def fused_call(nx, ny, spans, total, chunks, outs, *args):
    block, cols, rows, short, geo, codes, counts, gd, gp, rw, emb, cw, owner = args
    slots, atoms = codes.shape
    species, channels = emb.shape
    directions, width = owner.shape
    scratch = [
        pltpu.VMEM((nx, ny) + block.shape, F32),
        pltpu.VMEM((nx, ny, channels, 2 * LANES), F32),
        pltpu.VMEM((rows.shape[0], 2, 2 * LANES, atoms), BF16),
        pltpu.VMEM((2 * LANES, 4 * channels), F32),
        pltpu.VMEM((2 * LANES, 2 * channels), F32),
        pltpu.VMEM((channels, atoms), F32),
        pltpu.VMEM((4 * channels, atoms), F32),
        pltpu.VMEM((3, slots, atoms), F32),
        pltpu.VMEM((slots, LANES, atoms), BF16),
        pltpu.VMEM((rw.shape[0], species, atoms), F32),
        pltpu.VMEM((6 * chunks, LANES), F32),
        pltpu.VMEM((directions, SUBLANES, width), F32),
        pltpu.VMEM((directions, SUBLANES, width), F32),
    ]
    scratch += spread_semaphores(nx, ny) + spread_semaphores(nx, ny)
    scratch += [pltpu.SemaphoreType.DMA((directions,)), pltpu.SemaphoreType.DMA((directions,))]
    return pl.pallas_call(
        functools.partial(fused_kernel, nx, ny, spans, total),
        name="charges_to_forces",
        out_shape=[jax.ShapeDtypeStruct(shape, F32) for shape in outs],
        in_specs=[pl.BlockSpec(memory_space=VMEM)] * len(args),
        out_specs=[pl.BlockSpec(memory_space=VMEM)] * len(outs),
        scratch_shapes=scratch,
        compiler_params=pltpu.CompilerParams(
            collective_id=1, has_side_effects=True, vmem_limit_bytes=VMEM_LIMIT
        ),
    )(*args)


def local_call(kernel, name, outs, scratch, *args):
    return pl.pallas_call(
        kernel,
        name=name,
        out_shape=[jax.ShapeDtypeStruct(shape, F32) for shape in outs],
        in_specs=[pl.BlockSpec(memory_space=VMEM)] * len(args),
        out_specs=[pl.BlockSpec(memory_space=VMEM)] * len(outs),
        scratch_shapes=[pltpu.VMEM(shape, F32) for shape in scratch],
        compiler_params=pltpu.CompilerParams(vmem_limit_bytes=VMEM_LIMIT),
    )(*args)


def on_device(
    positions,
    species,
    neighbours,
    counts,
    ghost_list,
    wave_index,
    embedding,
    radial_weight,
    product_weight,
    readout_weight,
    charge_weight,
):
    nx, ny = lax.axis_size("gx"), lax.axis_size("gy")
    domains = nx * ny
    atoms = positions.shape[3]
    codes = neighbours[0, 0]
    slots = codes.shape[0]
    used = counts[0]
    ghost_rows = ghost_list[0, 0]
    directions, width = ghost_rows.shape
    waves = wave_index.shape[1]
    kinds, channels = embedding.shape
    basis = radial_weight.shape[0]
    spans = (float(nx), float(ny), SLAB_HEIGHT)
    total_atoms = float(atoms * domains)
    gx, gy = lax.axis_index("gx"), lax.axis_index("gy")
    record = jnp.concatenate(
        [positions.reshape(3, atoms), species[0].astype(F32)], axis=0
    )
    anchor = jnp.stack([gx.astype(F32), gy.astype(F32), jnp.zeros((), F32)]).reshape(3, 1)
    wave_float = wave_index.astype(F32)
    wave_cols = wave_float.T
    wave_rows = jnp.pad(
        wave_float.reshape(3, waves // LANES, LANES).transpose(1, 0, 2), ((0, 0), (0, 5), (0, 0))
    )
    readout = readout_weight.reshape(channels, 1)

    (outgoing,) = local_call(
        pick_kernel, "pick_ghosts", [(directions, SUBLANES, width)], [], record, ghost_rows
    )
    ghosts = swap_blocks(outgoing, 1, nx, ny, 0)
    block, short_energy, geometry, density_grad, polar_grad = local_call(
        short_kernel,
        "short_range",
        [
            (channels + SUBLANES, atoms),
            (1, atoms),
            (5, slots, atoms),
            (basis * kinds, atoms),
            (3 * basis, kinds, atoms),
        ],
        [(4 * basis, slots, atoms), (4 * basis, kinds, atoms)],
        record, ghosts, codes, used, anchor,
        embedding, radial_weight, product_weight, readout, charge_weight,
    )
    wave_blocks = waves // LANES
    chunks = 16 * -(-(atoms // LANES + directions * width // LANES) // 16)
    if wave_blocks == domains:
        energy, forces = fused_call(
            nx, ny, spans, total_atoms, chunks, [(1, atoms), (3, atoms)],
            block, wave_cols, wave_rows, short_energy, geometry, codes, used,
            density_grad, polar_grad, radial_weight, embedding, charge_weight, ghost_rows,
        )
        return (forces[:, None, None, :], energy[None])
    charge_total = lax.psum(jnp.sum(block[:channels], axis=1, keepdims=True), ("gx", "gy"))
    mean = jnp.broadcast_to(charge_total / total_atoms, (channels, LANES))
    neutral = jnp.concatenate([block[:channels] - mean[:, :1], block[channels:]], axis=0)
    (struct,) = local_call(
        functools.partial(structure_kernel, total_atoms, channels, spans),
        "structure",
        [(wave_blocks, channels, 2 * LANES)],
        [],
        neutral,
        wave_cols,
        wave_rows,
    )
    struct = lax.psum(struct, ("gx", "gy"))
    energy, own_grad, ghost_grad = local_call(
        functools.partial(back_kernel, spans),
        "gradients",
        [(1, atoms), (SUBLANES, atoms), (directions, SUBLANES, width)],
        [(basis, kinds, atoms), (3, slots, atoms), (6 * chunks, LANES)],
        struct, wave_cols, wave_rows, block, mean, short_energy, geometry, codes, used,
        density_grad, polar_grad, radial_weight, embedding, charge_weight,
    )
    back = swap_blocks(ghost_grad, -1, nx, ny, 3)
    (forces,) = local_call(owners_kernel, "owners", [(3, atoms)], [], back, ghost_rows, own_grad)
    return (forces[:, None, None, :], energy[None])


def solution(mesh):
    in_specs = (
        P(None, ("group", "gx"), "gy", None),
        P(("group", "gx"), "gy", None),
        P(("group", "gx"), "gy", None, None),
        P(("group", "gx"), "gy", None),
        P(("group", "gx"), "gy", None, None),
        P(),
        P(),
        P(),
        P(),
        P(),
        P(),
    )
    out_specs = (P(None, ("group", "gx"), "gy", None), P(("group", "gx"), "gy", None))
    return jax.shard_map(
        on_device, mesh=mesh, in_specs=in_specs, out_specs=out_specs, check_vma=False
    )
```

```python
import functools
import math

import jax
import jax.numpy as jnp
import numpy as np
from jax import lax
from jax.experimental import pallas as pl
from jax.experimental.pallas import tpu as pltpu
from jax.sharding import PartitionSpec as P

DIRECTIONS = ((-1, -1), (-1, 0), (-1, 1), (0, -1), (0, 1), (1, -1), (1, 0), (1, 1))
SOFTENING = 0.01
BASIS_WIDTH = 2.0
BASIS_STEP = 0.35
SCREENING = 0.02
SLAB_HEIGHT = 2.0
PRECISE = lax.Precision.HIGHEST
MESH = pl.DeviceIdType.MESH
LANES = 128
SUBLANES = 8
VMEM_LIMIT = 40 * 1024 * 1024
F32 = jnp.float32
BF16 = jnp.bfloat16
VMEM = pltpu.VMEM


def half_turn_series(odd, terms):
    nodes = 0.125 * (1.0 + np.cos(np.pi * (np.arange(64) + 0.5) / 64))
    root = np.sqrt(nodes)
    values = np.sin(np.pi * root) / root if odd else np.cos(np.pi * root)
    series = np.polynomial.chebyshev.Chebyshev.fit(nodes, values, terms - 1, domain=[0.0, 0.25])
    return [float(c) for c in series.convert(kind=np.polynomial.Polynomial).coef]


SIN_SERIES = half_turn_series(True, 6)
COS_SERIES = half_turn_series(False, 6)


def horner(series, square):
    total = jnp.full_like(square, series[-1])
    for coefficient in reversed(series[:-1]):
        total = total * square + coefficient
    return total


def cos_sin_turns(turns):
    reduced = turns - jnp.round(turns)
    square = reduced * reduced
    half_sin = reduced * horner(SIN_SERIES, square)
    half_cos = horner(COS_SERIES, square)
    return 1.0 - 2.0 * (half_sin * half_sin), 2.0 * (half_sin * half_cos)


def dot_nn(a, b):
    return lax.dot_general(
        a, b, (((1,), (0,)), ((), ())), precision=PRECISE, preferred_element_type=F32
    )


def dot_tn(a, b):
    return lax.dot_general(
        a, b, (((0,), (0,)), ((), ())), precision=PRECISE, preferred_element_type=F32
    )


def split_bf16(value):
    high = value.astype(BF16)
    return high, (value - high.astype(F32)).astype(BF16)


def dot3(a, b, dims):
    a_high, a_low = split_bf16(a)
    b_high, b_low = split_bf16(b)
    dot = functools.partial(
        lax.dot_general, dimension_numbers=(dims, ((), ())), preferred_element_type=F32
    )
    return dot(a_high, b_high) + (dot(a_high, b_low) + dot(a_low, b_high))


def lookup(table_row, codes):
    rows = codes.shape[0]
    pieces = []
    for part in range(codes.shape[1] // LANES):
        code = codes[:, part * LANES : (part + 1) * LANES]
        low, high = code % LANES, code // LANES
        found = jnp.zeros((rows, LANES), F32)
        for chunk in range(table_row.shape[1] // LANES):
            table = jnp.broadcast_to(
                table_row[:, chunk * LANES : (chunk + 1) * LANES], (rows, LANES)
            )
            picked = jnp.take_along_axis(table, low, axis=1)
            found = jnp.where(high == chunk, picked, found)
        pieces.append(found)
    return jnp.concatenate(pieces, axis=1)


def pick_kernel(record_ref, rows_ref, out_ref):
    rows = rows_ref[...]
    for field in range(4):
        found = lookup(record_ref[field : field + 1, :], rows)
        for direction, shift in enumerate(DIRECTIONS):
            offset = float(shift[field]) if field < 2 else 0.0
            out_ref[direction, field : field + 1, :] = found[direction : direction + 1] - offset
    for direction in range(len(DIRECTIONS)):
        out_ref[direction, 4:, :] = jnp.zeros((4, rows.shape[1]), F32)


def swap_kernel(sign, nx, ny, in_ref, out_ref, send_sem, recv_sem):
    gx, gy = lax.axis_index("gx"), lax.axis_index("gy")
    targets = [
        {
            "gx": lax.rem(gx + sign * sx + nx, nx),
            "gy": lax.rem(gy + sign * sy + ny, ny),
        }
        for sx, sy in DIRECTIONS
    ]
    barrier = pltpu.get_barrier_semaphore()
    for target in targets:
        pl.semaphore_signal(barrier, inc=1, device_id=target, device_id_type=MESH)
    pl.semaphore_wait(barrier, len(targets))
    copies = [
        pltpu.make_async_remote_copy(
            src_ref=in_ref.at[d],
            dst_ref=out_ref.at[d],
            send_sem=send_sem.at[d],
            recv_sem=recv_sem.at[d],
            device_id=target,
            device_id_type=MESH,
        )
        for d, target in enumerate(targets)
    ]
    for copy in copies:
        copy.start()
    for copy in copies:
        copy.wait()


def swap_blocks(blocks, sign, nx, ny, collective_id):
    count = blocks.shape[0]
    return pl.pallas_call(
        functools.partial(swap_kernel, sign, nx, ny),
        name="ghosts_out" if sign == 1 else "ghosts_back",
        out_shape=jax.ShapeDtypeStruct(blocks.shape, F32),
        in_specs=[pl.BlockSpec(memory_space=VMEM)],
        out_specs=pl.BlockSpec(memory_space=VMEM),
        scratch_shapes=[pltpu.SemaphoreType.DMA((count,)), pltpu.SemaphoreType.DMA((count,))],
        compiler_params=pltpu.CompilerParams(collective_id=collective_id, has_side_effects=True),
    )(blocks)


def mixing_of(radial_weight, embedding):
    return jnp.concatenate(
        [radial_weight[b : b + 1, :] * embedding for b in range(radial_weight.shape[0])], axis=0
    )


def short_kernel(
    record_ref, ghost_ref, codes_ref, counts_ref, anchor_ref,
    emb_ref, rw_ref, pw_ref, ro_ref, cw_ref,
    block_ref, energy_ref, geo_ref, gd_ref, gp_ref,
    terms_ref, moments_ref,
):
    slots, atoms = codes_ref.shape
    species, channels = emb_ref.shape
    basis = rw_ref.shape[0]
    codes = codes_ref[...]
    near = []
    for field in range(4):
        row = jnp.concatenate(
            [record_ref[field : field + 1, :]]
            + [ghost_ref[d, field : field + 1, :] for d in range(ghost_ref.shape[0])],
            axis=1,
        )
        near.append(lookup(row, codes))
    separation = [near[x] - record_ref[x : x + 1, :] for x in range(3)]
    square = separation[0] * separation[0]
    square = square + separation[1] * separation[1] + separation[2] * separation[2]
    radius = jnp.sqrt(square + SOFTENING)
    inverse = 1.0 / radius
    kind = near[3]
    slot = lax.broadcasted_iota(jnp.int32, (slots, atoms), 0)
    live = jnp.where(slot < counts_ref[...], 1.0, 0.0)
    unit = [part * inverse for part in separation]
    for x in range(3):
        geo_ref[x] = unit[x]
    geo_ref[3] = radius
    geo_ref[4] = kind
    for b in range(basis):
        offset = radius - BASIS_STEP * b
        radial = jnp.exp(-BASIS_WIDTH * (offset * offset)) * live
        terms_ref[b] = radial
        for x in range(3):
            terms_ref[(x + 1) * basis + b] = unit[x] * radial

    def reduce_term(q, carry):
        term = terms_ref[q]
        near_kind = geo_ref[4]
        rows = [
            jnp.sum(jnp.where(near_kind == float(s), term, 0.0), axis=0, keepdims=True)
            for s in range(species)
        ]
        moments_ref[q] = jnp.concatenate(rows, axis=0)
        return carry

    lax.fori_loop(0, 4 * basis, reduce_term, 0, unroll=2)
    mixing = mixing_of(rw_ref[...], emb_ref[...])
    norm = 1.0 / math.sqrt(slots)
    moments = [
        moments_ref[q * basis : (q + 1) * basis].reshape(basis * species, atoms) for q in range(4)
    ]
    own_species = lax.broadcasted_iota(jnp.int32, (species, atoms), 0).astype(F32)
    onehot = jnp.where(own_species == record_ref[3:4, :], 1.0, 0.0)
    scalar = norm * dot_tn(mixing, moments[0]) + dot_tn(emb_ref[...], onehot)
    vectorial = [norm * dot_tn(mixing, moments[x + 1]) for x in range(3)]
    squares = vectorial[0] * vectorial[0] + vectorial[1] * vectorial[1] + vectorial[2] * vectorial[2]
    invariants = jnp.concatenate([scalar, squares], axis=0)
    before = dot_tn(pw_ref[...], invariants)
    gate = 1.0 / (1.0 + jnp.exp(-before))
    hidden = before * gate
    energy_ref[...] = jnp.sum(hidden * ro_ref[...], axis=0, keepdims=True)
    block_ref[:channels, :] = dot_tn(cw_ref[...], scalar)
    block_ref[channels : channels + 3, :] = record_ref[:3, :] + anchor_ref[...]
    block_ref[channels + 3 :, :] = jnp.zeros((SUBLANES - 3, atoms), F32)
    slope = ro_ref[...] * (gate + hidden * (1.0 - gate))
    back = dot_nn(pw_ref[...], slope)
    gd_ref[...] = norm * dot_nn(mixing, back[:channels])
    for x in range(3):
        grad = norm * dot_nn(mixing, 2.0 * vectorial[x] * back[channels:])
        gp_ref[x * basis : (x + 1) * basis] = grad.reshape(basis, species, atoms)


def structure_kernel(total, channels, spans, block_ref, cols_ref, rows_ref, out_ref):
    def one_block(w, carry):
        cols = cols_ref[pl.ds(pl.multiple_of(w * LANES, LANES), LANES), :]
        turns = jnp.zeros((LANES, block_ref.shape[1]), F32)
        for x in range(3):
            placed = block_ref[channels + x : channels + x + 1, :]
            turns = turns + cols[:, x : x + 1] * (placed * (1.0 / spans[x]))
        waves = jnp.concatenate(cos_sin_turns(turns), axis=0)
        rows = rows_ref[w]
        squared = jnp.zeros((1, LANES), F32)
        for x in range(3):
            wave = rows[x : x + 1] * (2.0 * math.pi / spans[x])
            squared = squared + wave * wave
        weight = jnp.exp(-0.5 * SCREENING * SCREENING * squared) / (squared + 1.0)
        weight = weight * (1.0 / math.sqrt(total))
        factors = dot3(block_ref[:channels, :], waves, ((1,), (1,)))
        out_ref[w] = factors * jnp.concatenate([weight, weight], axis=1)
        return carry

    lax.fori_loop(0, out_ref.shape[0], one_block, 0)


def back_kernel(
    spans, struct_ref, cols_ref, rows_ref, block_ref, mean_ref, short_ref, geo_ref, codes_ref,
    counts_ref, gd_ref, gp_ref, rw_ref, emb_ref, cw_ref,
    energy_ref, own_ref, ghost_ref,
    gd_rows_ref, pair_ref, acc_ref,
):
    slots, atoms = codes_ref.shape
    species, channels = emb_ref.shape
    basis = rw_ref.shape[0]
    wave_blocks = struct_ref.shape[0]
    neutral = block_ref[:channels, :] - mean_ref[:, 0:1]
    neutral_high, neutral_low = split_bf16(neutral)
    scaled = [block_ref[channels + x : channels + x + 1, :] * (1.0 / spans[x]) for x in range(3)]
    over_rows = ((0,), (0,))

    def add_waves(w, carry):
        potential, pulled = carry
        cols = cols_ref[pl.ds(pl.multiple_of(w * LANES, LANES), LANES), :]
        turns = cols[:, 0:1] * scaled[0] + cols[:, 1:2] * scaled[1] + cols[:, 2:3] * scaled[2]
        cosine, sine = cos_sin_turns(turns)
        waves = jnp.concatenate([cosine, sine], axis=0)
        struct = struct_ref[w]
        potential = potential + dot3(struct, waves, ((1,), (0,)))
        high, low = split_bf16(struct)
        dot = functools.partial(
            lax.dot_general, dimension_numbers=(over_rows, ((), ())), preferred_element_type=F32
        )
        projected = dot(high, neutral_high) + (dot(high, neutral_low) + dot(low, neutral_high))
        torque = cosine * projected[LANES:] - sine * projected[:LANES]
        return potential, pulled + dot3(rows_ref[w], torque, ((1,), (0,)))

    potential, pulled = lax.fori_loop(
        0,
        wave_blocks,
        add_waves,
        (jnp.zeros((channels, atoms), F32), jnp.zeros((SUBLANES, atoms), F32)),
    )
    energy_ref[...] = short_ref[...] + 0.5 * jnp.sum(neutral * potential, axis=0, keepdims=True)
    mixing = mixing_of(rw_ref[...], emb_ref[...])
    norm = 1.0 / math.sqrt(slots)
    density_grad = gd_ref[...] + norm * dot_nn(mixing, dot_nn(cw_ref[...], potential))
    gd_rows_ref[...] = density_grad.reshape(basis, species, atoms)

    def pair_rows(i, carry):
        start = pl.multiple_of(i * SUBLANES, SUBLANES)
        window = pl.ds(start, SUBLANES)
        unit = [geo_ref[x, window, :] for x in range(3)]
        radius = geo_ref[3, window, :]
        kind = geo_ref[4, window, :]
        masks = [kind == float(s) for s in range(1, species)]
        slot = lax.broadcasted_iota(jnp.int32, (SUBLANES, atoms), 0) + start
        live = jnp.where(slot < counts_ref[...], 1.0, 0.0)

        def of_kind(table):
            chosen = jnp.broadcast_to(table[0:1, :], (SUBLANES, atoms))
            for s in range(1, species):
                chosen = jnp.where(masks[s - 1], table[s : s + 1, :], chosen)
            return chosen

        along = jnp.zeros((SUBLANES, atoms), F32)
        turn = [jnp.zeros((SUBLANES, atoms), F32) for x in range(3)]
        for b in range(basis):
            offset = radius - BASIS_STEP * b
            radial = jnp.exp(-BASIS_WIDTH * (offset * offset)) * live
            total = of_kind(gd_rows_ref[b])
            for x in range(3):
                polar = of_kind(gp_ref[x * basis + b])
                total = total + unit[x] * polar
                turn[x] = turn[x] + radial * polar
            along = along + (-2.0 * BASIS_WIDTH) * offset * radial * total
        inverse = 1.0 / radius
        swing = turn[0] * unit[0] + turn[1] * unit[1] + turn[2] * unit[2]
        radial_part = along - swing * inverse
        for x in range(3):
            pair_ref[x, window, :] = unit[x] * radial_part + turn[x] * inverse
        return carry

    lax.fori_loop(0, slots // SUBLANES, pair_rows, 0)
    chunks = acc_ref.shape[0] // 6
    acc_ref[...] = jnp.zeros(acc_ref.shape, F32)
    group = 4

    def scatter_rows(i, carry):
        start = i * group
        total = None
        for k in range(group):
            code = codes_ref[pl.ds(start + k, 1), :]
            low, high = code % LANES, code // LANES
            spots = lax.broadcasted_iota(jnp.int32, (LANES, atoms), 0)
            onehot = jnp.where(spots == low, 1.0, 0.0).astype(BF16)
            chunk_ids = lax.broadcasted_iota(jnp.int32, (chunks, atoms), 0)
            here = chunk_ids == high
            values = jnp.concatenate(
                [jnp.where(here, pair_ref[x, pl.ds(start + k, 1), :], 0.0) for x in range(3)],
                axis=0,
            )
            values = jnp.concatenate(split_bf16(values), axis=0)
            part = lax.dot_general(
                values, onehot, (((1,), (1,)), ((), ())), preferred_element_type=F32
            )
            total = part if total is None else total + part
        acc_ref[...] += total
        return carry

    lax.fori_loop(0, slots // group, scatter_rows, 0)
    summed = acc_ref[: 3 * chunks, :] + acc_ref[3 * chunks :, :]
    own_chunks = atoms // LANES
    own_ref[...] = jnp.zeros(own_ref.shape, F32)
    ghost_ref[...] = jnp.zeros(ghost_ref.shape, F32)
    for x in range(3):
        received = jnp.concatenate(
            [summed[x * chunks + h : x * chunks + h + 1, :] for h in range(own_chunks)], axis=1
        )
        centre = jnp.sum(pair_ref[x], axis=0, keepdims=True)
        wave_pull = pulled[x : x + 1, :] * (2.0 * math.pi / spans[x])
        own_ref[x : x + 1, :] = received - centre + wave_pull
        for d in range(ghost_ref.shape[0]):
            row = x * chunks + own_chunks + d
            ghost_ref[d, x : x + 1, :] = summed[row : row + 1, :]


def owned(values, rows, atoms):
    ids = lax.broadcasted_iota(jnp.int32, (atoms, rows.shape[1]), 0)
    onehot = jnp.where(ids == rows, 1.0, 0.0).astype(BF16)
    halves = jnp.concatenate(split_bf16(values), axis=0)
    part = lax.dot_general(halves, onehot, (((1,), (1,)), ((), ())), preferred_element_type=F32)
    return part[:SUBLANES] + part[SUBLANES:]


def owners_kernel(back_ref, rows_ref, own_ref, out_ref):
    total = own_ref[...]
    for d in range(back_ref.shape[0]):
        total = total + owned(back_ref[d], rows_ref[d : d + 1, :], own_ref.shape[1])
    out_ref[...] = -total[:3]


class Spread:
    def __init__(self, nx, ny, buffer, line_sem, cross_sem, pair_sem, recv_sem):
        self.gx, self.gy = lax.axis_index("gx"), lax.axis_index("gy")
        self.nx, self.chips = nx, ny // 2
        self.core = lax.rem(self.gy, 2)
        self.chip = self.gy // 2
        self.peer = self.chip * 2 + (1 - self.core)
        order = sorted(range(1, nx), key=lambda step: min(step, nx - step))
        self.lines = [lax.rem(self.gx + step, nx) for step in order]
        self.crosses = [
            lax.rem(self.chip + step, self.chips) * 2 + self.core for step in range(1, self.chips)
        ]
        self.buffer = buffer
        self.line_sem, self.cross_sem, self.pair_sem = line_sem, cross_sem, pair_sem
        self.recv_sem = recv_sem
        self.sent = []

    def remote(self, x, y, send_sem, device):
        return pltpu.make_async_remote_copy(
            src_ref=self.buffer.at[x, y],
            dst_ref=self.buffer.at[x, y],
            send_sem=send_sem,
            recv_sem=self.recv_sem.at[x, y],
            device_id=device,
            device_id_type=MESH,
        )

    def send(self, x, y, send_sem, device):
        copy = self.remote(x, y, send_sem, device)
        copy.start()
        self.sent.append(copy)

    def arrived(self, x, y):
        self.remote(x, y, self.line_sem.at[0], {"gy": self.peer}).wait_recv()

    def to_chip(self, x, row):
        for index, y in enumerate(self.crosses):
            self.send(x, self.gy, self.cross_sem.at[row, index], {"gy": y})
        self.send(x, self.gy, self.pair_sem.at[row, 0], {"gy": self.peer})

    def start(self):
        for index, x in enumerate(self.lines):
            self.send(self.gx, self.gy, self.line_sem.at[index], {"gx": x})
        self.to_chip(self.gx, 0)

    def take_lines(self, beside):
        for row, x in enumerate(self.lines):
            self.arrived(x, self.gy)
            self.to_chip(x, row + 1)
            beside(row, x, self.gy)

    def take_crosses(self, beside):
        for row, x in enumerate([self.gx] + self.lines):
            for index, y in enumerate(self.crosses):
                self.arrived(x, y)
                self.send(x, y, self.pair_sem.at[row, index + 1], {"gy": self.peer})
                beside(row, x, y)

    def take_pairs(self, beside, first, last):
        count = last - first

        def one(j, carry):
            x = lax.rem(self.gx + j // count, self.nx)
            y = lax.rem(self.chip + first + j % count, self.chips) * 2 + (1 - self.core)
            self.arrived(x, y)
            beside(x, y)
            return carry

        if count > 0:
            lax.fori_loop(0, self.nx * count, one, 0)

    def finish(self):
        for copy in self.sent:
            copy.wait_send()


def fused_kernel(
    nx, ny, spans, total, block_ref, cols_ref, rows_ref, short_ref, geo_ref, codes_ref,
    counts_ref, gd_ref, gp_ref, rw_ref, emb_ref, cw_ref, owner_ref,
    energy_ref, force_ref,
    charge_ref, struct_ref, waves_ref, wide_ref, slim_ref, sum_ref, long_ref, pair_ref, onehot_ref, gd_rows_ref,
    acc_ref, ghost_ref, back_ref,
    line1, cross1, pair1, recv1, line2, cross2, pair2, recv2, swap_send, swap_recv,
):
    slots, atoms = codes_ref.shape
    species, channels = emb_ref.shape
    basis = rw_ref.shape[0]
    wave_blocks = rows_ref.shape[0]
    gx, gy = lax.axis_index("gx"), lax.axis_index("gy")
    mine = gx * ny + gy

    def other(sx, sy):
        return {"gx": lax.rem(gx + sx + nx, nx), "gy": lax.rem(gy + sy + ny, ny)}

    barrier = pltpu.get_barrier_semaphore()
    steps = {(sx, 0) for sx in range(1, nx)} | {(0, sy) for sy in range(1, ny)}
    steps |= {(sx % nx, sy % ny) for sx, sy in DIRECTIONS}
    for sx, sy in sorted(steps):
        pl.semaphore_signal(barrier, inc=1, device_id=other(sx, sy), device_id_type=MESH)
    charge_ref[gx, gy] = block_ref[...]
    pl.semaphore_wait(barrier, len(steps))
    first = Spread(nx, ny, charge_ref, line1, cross1, pair1, recv1)
    second = Spread(nx, ny, struct_ref, line2, cross2, pair2, recv2)
    first.start()

    def table(cols, placed):
        turns = cols[:, 0:1] * (placed[0:1] * (1.0 / spans[0]))
        turns = turns + cols[:, 1:2] * (placed[1:2] * (1.0 / spans[1]))
        turns = turns + cols[:, 2:3] * (placed[2:3] * (1.0 / spans[2]))
        cosine, sine = cos_sin_turns(turns)
        return split_bf16(jnp.concatenate([cosine, sine], axis=0))

    own_placed = block_ref[channels:, :]

    def own_waves(w, carry):
        cols = cols_ref[pl.ds(pl.multiple_of(w * LANES, LANES), LANES), :]
        high, low = table(cols, own_placed)
        waves_ref[w, 0] = high
        waves_ref[w, 1] = low
        return carry

    shift = jnp.sum(block_ref[:channels, :], axis=1, keepdims=True) * (1.0 / atoms)
    ones = jnp.ones((channels, atoms), BF16)
    blank = jnp.zeros((channels, atoms), BF16)
    wide_ref[...] = jnp.zeros(wide_ref.shape, F32)
    slim_ref[...] = jnp.zeros(slim_ref.shape, F32)
    sum_ref[...] = jnp.zeros(sum_ref.shape, F32)

    def over_atoms(a, b):
        return lax.dot_general(a, b, (((1,), (1,)), ((), ())), preferred_element_type=F32)

    def slice_waves(x, y):
        cols = cols_ref[pl.ds(pl.multiple_of(mine * LANES, LANES), LANES), :]
        high, low = table(cols, charge_ref[x, y, channels:, :])
        charges = charge_ref[x, y, :channels, :]
        sum_ref[...] += charges
        q_high, q_low = split_bf16(charges - shift)
        wide_ref[...] += over_atoms(high, jnp.concatenate([q_high, ones, q_low, blank], axis=0))
        slim_ref[...] += over_atoms(low, jnp.concatenate([q_high, ones], axis=0))

    slice_waves(gx, gy)
    early = wave_blocks * 3 // 8
    lax.fori_loop(0, early, own_waves, 0)
    first.take_lines(lambda row, x, y: slice_waves(x, y))

    def charge_cross(row, x, y):
        slice_waves(x, y)
        if row == nx - 2:
            first.take_pairs(slice_waves, 0, 1)

    first.take_crosses(charge_cross)
    first.take_pairs(slice_waves, 1, ny // 2)

    mean = jnp.sum(sum_ref[...], axis=1, keepdims=True) / total
    wide = wide_ref[...]
    main = jnp.transpose(wide[:, : 2 * channels] + slim_ref[...])
    rest = jnp.transpose(wide[:, 2 * channels :])
    factors = main[:channels] + rest[:channels]
    factors = factors + (shift - mean) * main[channels : channels + 1]
    rows = rows_ref[mine]
    squared = jnp.zeros((1, LANES), F32)
    for x in range(3):
        wave = rows[x : x + 1] * (2.0 * math.pi / spans[x])
        squared = squared + wave * wave
    weight = jnp.exp(-0.5 * SCREENING * SCREENING * squared) / (squared + 1.0)
    weight = weight * (1.0 / math.sqrt(total))
    struct_ref[gx, gy] = factors * jnp.concatenate([weight, weight], axis=1)
    second.start()

    def near_rows(i):
        start = pl.multiple_of(i * SUBLANES, SUBLANES)
        window = pl.ds(start, SUBLANES)
        unit = [geo_ref[x, window, :] for x in range(3)]
        radius = geo_ref[3, window, :]
        kind = geo_ref[4, window, :]
        masks = [kind == float(s) for s in range(1, species)]
        slot = lax.broadcasted_iota(jnp.int32, (SUBLANES, atoms), 0) + start
        live = jnp.where(slot < counts_ref[...], 1.0, 0.0)

        def of_kind(rows):
            chosen = jnp.broadcast_to(rows[0:1, :], (SUBLANES, atoms))
            for s in range(1, species):
                chosen = jnp.where(masks[s - 1], rows[s : s + 1, :], chosen)
            return chosen

        def radial_of(b):
            offset = radius - BASIS_STEP * b
            radial = jnp.exp(-BASIS_WIDTH * (offset * offset)) * live
            return radial, (-2.0 * BASIS_WIDTH) * offset * radial

        return window, unit, radius, of_kind, radial_of

    gd_rows_ref[...] = gd_ref[...].reshape(basis, species, atoms)

    def short_pairs(i, carry):
        window, unit, radius, of_kind, radial_of = near_rows(i)
        along = jnp.zeros((SUBLANES, atoms), F32)
        turn = [jnp.zeros((SUBLANES, atoms), F32) for x in range(3)]
        for b in range(basis):
            radial, slope = radial_of(b)
            whole = of_kind(gd_rows_ref[b])
            for x in range(3):
                polar = of_kind(gp_ref[x * basis + b])
                whole = whole + unit[x] * polar
                turn[x] = turn[x] + radial * polar
            along = along + slope * whole
        inverse = 1.0 / radius
        swing = turn[0] * unit[0] + turn[1] * unit[1] + turn[2] * unit[2]
        radial_part = along - swing * inverse
        for x in range(3):
            pair_ref[x, window, :] = unit[x] * radial_part + turn[x] * inverse
        return carry

    def spots(n, carry):
        low = codes_ref[pl.ds(n, 1), :] % LANES
        ids = lax.broadcasted_iota(jnp.int32, (LANES, atoms), 0)
        onehot_ref[n] = jnp.where(ids == low, 1.0, 0.0).astype(BF16)
        return carry

    cuts = [early + (wave_blocks - early) * k // nx for k in range(nx + 1)]
    lax.fori_loop(cuts[0], cuts[1], own_waves, 0)
    second.take_lines(
        lambda row, x, y: lax.fori_loop(cuts[row + 1], cuts[row + 2], own_waves, 0)
    )
    groups = slots // SUBLANES
    neutral = block_ref[:channels, :] - mean
    long_ref[...] = jnp.zeros(long_ref.shape, F32)

    def add_waves(x, y):
        w = x * ny + y
        struct = struct_ref[x, y]
        turned = jnp.concatenate([struct[:, LANES:], -struct[:, :LANES]], axis=1)
        rows = rows_ref[w]
        rows = jnp.concatenate([rows, rows], axis=1)
        parts = [struct] + [turned * rows[axis : axis + 1] for axis in range(3)]
        high, low = split_bf16(jnp.concatenate(parts, axis=0))
        both = jnp.dot(
            jnp.concatenate([high, low], axis=0), waves_ref[w, 0], preferred_element_type=F32
        )
        fine = jnp.dot(high, waves_ref[w, 1], preferred_element_type=F32)
        count = high.shape[0]
        long_ref[...] += both[:count] + both[count:] + fine

    chips = ny // 2
    core, chip = lax.rem(gy, 2), gy // 2

    def same_core(first_chip, last_chip):
        count = last_chip - first_chip

        def one(j, carry):
            x = lax.rem(gx + j // count, nx)
            add_waves(x, lax.rem(chip + first_chip + j % count, chips) * 2 + core)
            return carry

        if count > 0:
            lax.fori_loop(0, nx * count, one, 0)

    tasks = [
        lambda: lax.fori_loop(0, groups, short_pairs, 0),
        lambda: (lax.fori_loop(0, slots, spots, 0, unroll=2), same_core(0, 1)),
        lambda: second.take_pairs(add_waves, 0, 1),
    ]

    def struct_cross(row, x, y):
        if tasks:
            tasks.pop(0)()

    second.take_crosses(struct_cross)
    for task in tasks:
        task()
    same_core(1, chips)
    second.take_pairs(add_waves, 1, chips)
    potential = long_ref[:channels, :]
    pulled = [
        jnp.sum(neutral * long_ref[(x + 1) * channels : (x + 2) * channels, :], axis=0, keepdims=True)
        for x in range(3)
    ]

    energy_ref[...] = short_ref[...] + 0.5 * jnp.sum(neutral * potential, axis=0, keepdims=True)
    mixing = mixing_of(rw_ref[...], emb_ref[...])
    norm = 1.0 / math.sqrt(slots)
    density_grad = norm * dot_nn(mixing, dot_nn(cw_ref[...], potential))
    gd_rows_ref[...] = density_grad.reshape(basis, species, atoms)
    chunks = acc_ref.shape[0] // 6
    acc_ref[...] = jnp.zeros(acc_ref.shape, F32)
    chunk_ids = lax.broadcasted_iota(jnp.int32, (chunks, atoms), 0)

    def scatter_rows(i, centres):
        window, unit, radius, of_kind, radial_of = near_rows(i)
        along = jnp.zeros((SUBLANES, atoms), F32)
        for b in range(basis):
            along = along + radial_of(b)[1] * of_kind(gd_rows_ref[b])
        grads = [pair_ref[x, window, :] + unit[x] * along for x in range(3)]
        added = None
        high_codes = codes_ref[window, :] // LANES
        for k in range(SUBLANES):
            here = chunk_ids == high_codes[k : k + 1, :]
            values = jnp.concatenate(
                [jnp.where(here, grads[x][k : k + 1, :], 0.0) for x in range(3)], axis=0
            )
            part = lax.dot_general(
                jnp.concatenate(split_bf16(values), axis=0),
                onehot_ref[i * SUBLANES + k],
                (((1,), (1,)), ((), ())),
                preferred_element_type=F32,
            )
            added = part if added is None else added + part
        acc_ref[...] += added
        return tuple(centre + grad for centre, grad in zip(centres, grads))

    centres = lax.fori_loop(
        0, groups, scatter_rows, tuple(jnp.zeros((SUBLANES, atoms), F32) for x in range(3))
    )
    acc = acc_ref[: 3 * chunks, :] + acc_ref[3 * chunks :, :]
    own_chunks = atoms // LANES
    for d in range(len(DIRECTIONS)):
        picked = [acc[x * chunks + own_chunks + d : x * chunks + own_chunks + d + 1] for x in range(3)]
        filler = jnp.zeros((SUBLANES - 3, ghost_ref.shape[2]), F32)
        ghost_ref[d] = jnp.concatenate(picked + [filler], axis=0)
    swaps = [
        pltpu.make_async_remote_copy(
            src_ref=ghost_ref.at[d],
            dst_ref=back_ref.at[d],
            send_sem=swap_send.at[d],
            recv_sem=swap_recv.at[d],
            device_id=other(-sx, -sy),
            device_id_type=MESH,
        )
        for d, (sx, sy) in enumerate(DIRECTIONS)
    ]
    for swap in swaps:
        swap.start()
    rows = []
    for x in range(3):
        received = jnp.concatenate(
            [acc[x * chunks + h : x * chunks + h + 1, :] for h in range(own_chunks)], axis=1
        )
        centre = jnp.sum(centres[x], axis=0, keepdims=True)
        rows.append(received - centre + pulled[x] * (2.0 * math.pi / spans[x]))
    sums = jnp.concatenate(rows + [jnp.zeros((SUBLANES - 3, atoms), F32)], axis=0)
    first.finish()
    second.finish()
    for d, swap in enumerate(swaps):
        swap.wait()
        sums = sums + owned(back_ref[d], owner_ref[d : d + 1, :], atoms)
    force_ref[...] = -sums[:3]


def spread_semaphores(nx, ny):
    chips = ny // 2
    return [
        pltpu.SemaphoreType.DMA((nx - 1,)),
        pltpu.SemaphoreType.DMA((nx, max(chips - 1, 1))),
        pltpu.SemaphoreType.DMA((nx, chips)),
        pltpu.SemaphoreType.DMA((nx, ny)),
    ]


def fused_call(nx, ny, spans, total, chunks, outs, *args):
    block, cols, rows, short, geo, codes, counts, gd, gp, rw, emb, cw, owner = args
    slots, atoms = codes.shape
    species, channels = emb.shape
    directions, width = owner.shape
    scratch = [
        pltpu.VMEM((nx, ny) + block.shape, F32),
        pltpu.VMEM((nx, ny, channels, 2 * LANES), F32),
        pltpu.VMEM((rows.shape[0], 2, 2 * LANES, atoms), BF16),
        pltpu.VMEM((2 * LANES, 4 * channels), F32),
        pltpu.VMEM((2 * LANES, 2 * channels), F32),
        pltpu.VMEM((channels, atoms), F32),
        pltpu.VMEM((4 * channels, atoms), F32),
        pltpu.VMEM((3, slots, atoms), F32),
        pltpu.VMEM((slots, LANES, atoms), BF16),
        pltpu.VMEM((rw.shape[0], species, atoms), F32),
        pltpu.VMEM((6 * chunks, LANES), F32),
        pltpu.VMEM((directions, SUBLANES, width), F32),
        pltpu.VMEM((directions, SUBLANES, width), F32),
    ]
    scratch += spread_semaphores(nx, ny) + spread_semaphores(nx, ny)
    scratch += [pltpu.SemaphoreType.DMA((directions,)), pltpu.SemaphoreType.DMA((directions,))]
    return pl.pallas_call(
        functools.partial(fused_kernel, nx, ny, spans, total),
        name="charges_to_forces",
        out_shape=[jax.ShapeDtypeStruct(shape, F32) for shape in outs],
        in_specs=[pl.BlockSpec(memory_space=VMEM)] * len(args),
        out_specs=[pl.BlockSpec(memory_space=VMEM)] * len(outs),
        scratch_shapes=scratch,
        compiler_params=pltpu.CompilerParams(
            collective_id=1, has_side_effects=True, vmem_limit_bytes=VMEM_LIMIT
        ),
    )(*args)


def local_call(kernel, name, outs, scratch, *args):
    return pl.pallas_call(
        kernel,
        name=name,
        out_shape=[jax.ShapeDtypeStruct(shape, F32) for shape in outs],
        in_specs=[pl.BlockSpec(memory_space=VMEM)] * len(args),
        out_specs=[pl.BlockSpec(memory_space=VMEM)] * len(outs),
        scratch_shapes=[pltpu.VMEM(shape, F32) for shape in scratch],
        compiler_params=pltpu.CompilerParams(vmem_limit_bytes=VMEM_LIMIT),
    )(*args)


def on_device(
    positions,
    species,
    neighbours,
    counts,
    ghost_list,
    wave_index,
    embedding,
    radial_weight,
    product_weight,
    readout_weight,
    charge_weight,
):
    nx, ny = lax.axis_size("gx"), lax.axis_size("gy")
    domains = nx * ny
    atoms = positions.shape[3]
    codes = neighbours[0, 0]
    slots = codes.shape[0]
    used = counts[0]
    ghost_rows = ghost_list[0, 0]
    directions, width = ghost_rows.shape
    waves = wave_index.shape[1]
    kinds, channels = embedding.shape
    basis = radial_weight.shape[0]
    spans = (float(nx), float(ny), SLAB_HEIGHT)
    total_atoms = float(atoms * domains)
    gx, gy = lax.axis_index("gx"), lax.axis_index("gy")
    record = jnp.concatenate(
        [positions.reshape(3, atoms), species[0].astype(F32)], axis=0
    )
    anchor = jnp.stack([gx.astype(F32), gy.astype(F32), jnp.zeros((), F32)]).reshape(3, 1)
    wave_float = wave_index.astype(F32)
    wave_cols = wave_float.T
    wave_rows = jnp.pad(
        wave_float.reshape(3, waves // LANES, LANES).transpose(1, 0, 2), ((0, 0), (0, 5), (0, 0))
    )
    readout = readout_weight.reshape(channels, 1)

    (outgoing,) = local_call(
        pick_kernel, "pick_ghosts", [(directions, SUBLANES, width)], [], record, ghost_rows
    )
    ghosts = swap_blocks(outgoing, 1, nx, ny, 0)
    block, short_energy, geometry, density_grad, polar_grad = local_call(
        short_kernel,
        "short_range",
        [
            (channels + SUBLANES, atoms),
            (1, atoms),
            (5, slots, atoms),
            (basis * kinds, atoms),
            (3 * basis, kinds, atoms),
        ],
        [(4 * basis, slots, atoms), (4 * basis, kinds, atoms)],
        record, ghosts, codes, used, anchor,
        embedding, radial_weight, product_weight, readout, charge_weight,
    )
    wave_blocks = waves // LANES
    chunks = 16 * -(-(atoms // LANES + directions * width // LANES) // 16)
    if wave_blocks == domains:
        energy, forces = fused_call(
            nx, ny, spans, total_atoms, chunks, [(1, atoms), (3, atoms)],
            block, wave_cols, wave_rows, short_energy, geometry, codes, used,
            density_grad, polar_grad, radial_weight, embedding, charge_weight, ghost_rows,
        )
        return (forces[:, None, None, :], energy[None])
    charge_total = lax.psum(jnp.sum(block[:channels], axis=1, keepdims=True), ("gx", "gy"))
    mean = jnp.broadcast_to(charge_total / total_atoms, (channels, LANES))
    neutral = jnp.concatenate([block[:channels] - mean[:, :1], block[channels:]], axis=0)
    (struct,) = local_call(
        functools.partial(structure_kernel, total_atoms, channels, spans),
        "structure",
        [(wave_blocks, channels, 2 * LANES)],
        [],
        neutral,
        wave_cols,
        wave_rows,
    )
    struct = lax.psum(struct, ("gx", "gy"))
    energy, own_grad, ghost_grad = local_call(
        functools.partial(back_kernel, spans),
        "gradients",
        [(1, atoms), (SUBLANES, atoms), (directions, SUBLANES, width)],
        [(basis, kinds, atoms), (3, slots, atoms), (6 * chunks, LANES)],
        struct, wave_cols, wave_rows, block, mean, short_energy, geometry, codes, used,
        density_grad, polar_grad, radial_weight, embedding, charge_weight,
    )
    back = swap_blocks(ghost_grad, -1, nx, ny, 3)
    (forces,) = local_call(owners_kernel, "owners", [(3, atoms)], [], back, ghost_rows, own_grad)
    return (forces[:, None, None, :], energy[None])


def solution(mesh):
    in_specs = (
        P(None, ("group", "gx"), "gy", None),
        P(("group", "gx"), "gy", None),
        P(("group", "gx"), "gy", None, None),
        P(("group", "gx"), "gy", None),
        P(("group", "gx"), "gy", None, None),
        P(),
        P(),
        P(),
        P(),
        P(),
        P(),
    )
    out_specs = (P(None, ("group", "gx"), "gy", None), P(("group", "gx"), "gy", None))
    return jax.shard_map(
        on_device, mesh=mesh, in_specs=in_specs, out_specs=out_specs, check_vma=False
    )
```
